256 devices in a mesh: section: 4 (over y_hi, core), expert: 32 (over x, z), narrow: 2 (over y_lo).
Axes of the slice: x: 4, y: 4 (y_hi: 2, y_lo: 2; y = y_hi * 2 + y_lo), z: 8, core: 2. Of those that a mesh axis runs over, the one named last changes fastest.
Arguments:
- ahead_tokens: bfloat16 [4, 8192, 3584], P('section', ('expert', 'narrow')), may hold values from -6 to 6
- ahead_routes: int32 [4, 8192, 1], P('section', ('expert', 'narrow')), may hold values from 0 to 15; in each aligned block of 128 rows (0 to 127, 128 to 255, ..., all dimensions but the last counted through in order) at most 10 rows name the same one
- ahead_weights: float32 [4, 8192, 1], P('section', ('expert', 'narrow')), may hold values from 0.1 to 1
- back_tokens: bfloat16 [4, 8192, 3584], P('section', ('expert', 'narrow')), may hold values from -6 to 6
- back_grads: bfloat16 [4, 8192, 3584], P('section', ('expert', 'narrow')), may hold values from -6 to 6
- back_routes: int32 [4, 8192, 1], P('section', ('expert', 'narrow')), may hold values from 0 to 15; in each aligned block of 128 rows (0 to 127, 128 to 255, ..., all dimensions but the last counted through in order) at most 10 rows name the same one
- back_weights: float32 [4, 8192, 1], P('section', ('expert', 'narrow')), may hold values from 0.1 to 1
- gate_weight: bfloat16 [4, 3584, 16384], P('section', None, ('expert', 'narrow')), may hold values from -0.09375 to 0.09375
- up_weight: bfloat16 [4, 3584, 16384], P('section', None, ('expert', 'narrow')), may hold values from -0.09375 to 0.09375
- down_weight: bfloat16 [4, 16384, 3584], P('section', ('expert', 'narrow')), may hold values from -0.1875 to 0.1875
Outputs:
- next_input: bfloat16 [4, 8192, 3584], P('section', ('expert', 'narrow'))
- prev_grad: bfloat16 [4, 8192, 3584], P('section', ('expert', 'narrow'))
The draws below stay inside these ranges and needn't reach their ends.
Inputs may be any that keep to these rules, and one draw needn't show every extreme that they name: `ahead_routes`: each token names 1 expert; among the 128 tokens of one device no expert is named more than 10 times, and in every draw some device's tokens name some expert exactly 10 times. `back_routes`: as for ahead_routes.
All inputs are finite; a program needn't handle non-finite values.
Results may differ from the reference program's by a relative error of at most 0.0057.
Values may be sent and summed in bfloat16 or wider, within the bound.
No kernel may reach another device: no remote copies, remote signals or barrier semaphores. Data moves between devices by JAX's collectives and lax.ppermute only.
A program may use at most 128 MiB of HBM per device.

```python
import math
import jax
import jax.numpy as jnp
import numpy as np

DW = 3584
HID = 1024
TOK_DEV = 128
TOPK = 1
SECTIONS = 4
EXPERTS = 16
CAP = 10
TOKENS = 8192


def block_levels(own_key, shape, shards, least, largest):
    factor_of = 1.0
    for position, blocks in shards:
        heights = jax.random.uniform(jax.random.fold_in(jax.random.fold_in(own_key, 6), position), (blocks,), jnp.float32, least / len(shards), largest / len(shards))
        factor_of = factor_of * jnp.repeat(jnp.exp(heights), shape[position] // blocks).reshape((-1,) + (1,) * (len(shape) - 1 - position))
    return factor_of


def routed_block(own_key, own, number, rows, amount, top, reach, skew):
    order = jax.random.permutation(own_key, amount)
    packed, common = portions_of(amount, rows * top, reach, skew, True), portions_of(amount, rows * top, reach, skew, False)
    places = jnp.arange(amount)

    def named(sizes, offset_by):
        used = int((sizes > 0).sum())
        fixed = max(1, used // 4)
        passed = fixed + (places - fixed + offset_by * (used - fixed)) % max(1, amount - fixed)
        return jnp.zeros((amount,), jnp.int32).at[order[jnp.where(places < fixed, places, passed)]].set(jnp.asarray(sizes, jnp.int32))

    sizes = jnp.where(number % 4 == 0, named(packed, number // 4), named(common, number - number // 4 - 1))
    mixed = jax.random.permutation(jax.random.fold_in(own, 3), amount)
    donor, receiver = mixed[0:amount // 2 * 2:2], mixed[1:amount // 2 * 2:2]
    margin = jnp.minimum(sizes[donor] - 1, reach - sizes[receiver]) // 2
    margin = jnp.where((donor == order[0]) | (receiver == order[0]) | (sizes[receiver] == 0), 0, jnp.maximum(margin, 0))
    passed = jax.random.randint(jax.random.fold_in(own, 4), (amount // 2,), 0, 1 << 20) % (margin + 1)
    sizes = sizes.at[donor].add(-passed).at[receiver].add(passed)
    items = jnp.searchsorted(jnp.cumsum(sizes), jnp.arange(rows * top), side="right").astype(jnp.int32)
    table = items.reshape(top, rows).T
    table = table[jax.random.permutation(jax.random.fold_in(own, 1), rows)]
    offset_by = jax.random.randint(jax.random.fold_in(own, 2), (rows, 1), 0, top)
    return jnp.take_along_axis(table, (jnp.arange(top)[None, :] + offset_by) % top, axis=1)


def portions_of(amount, total, most, lean, full):
    portions = [(1 << 20) // math.isqrt(rank ** lean) + 1 for rank in range(1, amount + 1)]
    largest = most if full else min(most, max(-(-total // amount), total * portions[0] // sum(portions)))
    least = 1 if total - largest >= amount - 1 else 0
    given, surplus = [largest] + [least] * (amount - 1), total - largest - least * (amount - 1)
    while surplus > 0:
        candidates = [i for i in range(1, amount) if given[i] < largest] or [i for i in range(1, amount) if given[i] < most]
        whole, left = sum([portions[i] for i in candidates]), surplus
        for i in candidates:
            extra = min(most - given[i], max(1, left * portions[i] // whole), surplus)
            given[i] = given[i] + extra
            surplus = surplus - extra
    return np.array(given)


def gaussian(own_key, extent, spread, reach, shards=(), dtype=jnp.bfloat16):
    array = spread * jax.random.normal(own_key, extent, jnp.float32)
    if shards:
        array = array * block_levels(own_key, extent, shards, -0.22, 0.18)
    return jnp.clip(array, -reach, reach).astype(dtype)


def setup_inputs(seed: int = 0) -> dict:
    streams_of = jax.random.split(jax.random.key(seed), 11)
    ahead_tokens = gaussian(streams_of[0], (SECTIONS, TOKENS, DW), 1.0, 6.0, ((0, 4), (1, 64)))
    ahead_routes_keys = jax.random.split(jax.random.fold_in(streams_of[1], 1), SECTIONS * TOKENS // TOK_DEV)
    ahead_routes_turns = jax.random.permutation(jax.random.fold_in(streams_of[1], 3), SECTIONS * TOKENS // TOK_DEV)
    ahead_routes = jax.vmap(lambda own, number: routed_block(jax.random.fold_in(streams_of[1], 2), own, number, TOK_DEV, EXPERTS, TOPK, CAP, 2))(ahead_routes_keys, ahead_routes_turns).reshape((SECTIONS, TOKENS, TOPK))
    ahead_weights = jnp.clip(0.1 + 0.9 * jax.random.uniform(streams_of[2], (SECTIONS, TOKENS, TOPK), jnp.float32) ** block_levels(streams_of[2], (SECTIONS, TOKENS, TOPK), ((0, 4), (1, 64)), -0.2, 0.2), 0.1, 1.0)
    back_tokens = gaussian(streams_of[3], (SECTIONS, TOKENS, DW), 1.0, 6.0, ((0, 4), (1, 64)))
    back_grads = gaussian(streams_of[4], (SECTIONS, TOKENS, DW), 1.0, 6.0, ((0, 4), (1, 64)))
    back_routes_keys = jax.random.split(jax.random.fold_in(streams_of[5], 1), SECTIONS * TOKENS // TOK_DEV)
    back_routes_turns = jax.random.permutation(jax.random.fold_in(streams_of[5], 3), SECTIONS * TOKENS // TOK_DEV)
    back_routes = jax.vmap(lambda own, number: routed_block(jax.random.fold_in(streams_of[5], 2), own, number, TOK_DEV, EXPERTS, TOPK, CAP, 2))(back_routes_keys, back_routes_turns).reshape((SECTIONS, TOKENS, TOPK))
    back_weights = jnp.clip(0.1 + 0.9 * jax.random.uniform(streams_of[6], (SECTIONS, TOKENS, TOPK), jnp.float32) ** block_levels(streams_of[6], (SECTIONS, TOKENS, TOPK), ((0, 4), (1, 64)), -0.2, 0.2), 0.1, 1.0)
    gate_weight = gaussian(streams_of[7], (SECTIONS, DW, EXPERTS * HID), DW ** -0.5, 0.09375, ((0, 4), (2, 64)))
    up_weight = gaussian(streams_of[8], (SECTIONS, DW, EXPERTS * HID), DW ** -0.5, 0.09375, ((0, 4), (2, 64)))
    down_weight = gaussian(streams_of[9], (SECTIONS, EXPERTS * HID, DW), HID ** -0.5, 0.1875, ((0, 4), (1, 64)))
    return dict(ahead_tokens=ahead_tokens, ahead_routes=ahead_routes, ahead_weights=ahead_weights, back_tokens=back_tokens, back_grads=back_grads, back_routes=back_routes, back_weights=back_weights, gate_weight=gate_weight, up_weight=up_weight, down_weight=down_weight)


def expert_forward(rows, gate_w, up_w, down_w):
    gate = jnp.dot(rows, gate_w, preferred_element_type=jnp.float32)
    up = jnp.dot(rows, up_w, preferred_element_type=jnp.float32)
    hidden = (jax.nn.silu(gate) * up).astype(jnp.bfloat16)
    return jnp.dot(hidden, down_w, preferred_element_type=jnp.float32).astype(jnp.bfloat16)


def expert_backward(rows, grads, gate_w, up_w, down_w):
    gate = jnp.dot(rows, gate_w, preferred_element_type=jnp.float32)
    up = jnp.dot(rows, up_w, preferred_element_type=jnp.float32)
    carried = jnp.dot(grads, down_w.T, preferred_element_type=jnp.float32)
    sigma = jax.nn.sigmoid(gate)
    d_gate = (carried * up * sigma * (1.0 + gate * (1.0 - sigma))).astype(jnp.bfloat16)
    d_up = (carried * gate * sigma).astype(jnp.bfloat16)
    total = jnp.dot(d_gate, gate_w.T, preferred_element_type=jnp.float32)
    total = total + jnp.dot(d_up, up_w.T, preferred_element_type=jnp.float32)
    return total.astype(jnp.bfloat16)


def reference(ahead_tokens, ahead_routes, ahead_weights, back_tokens, back_grads, back_routes, back_weights, gate_weight, up_weight, down_weight):
    layer_list = []
    grad_list = []
    for section in range(SECTIONS):
        layer_out = jnp.zeros((TOKENS, DW), jnp.float32)
        input_grad = jnp.zeros((TOKENS, DW), jnp.float32)
        for expert in range(EXPERTS):
            low = expert * HID
            gate_w = gate_weight[section][:, low:low + HID]
            up_w = up_weight[section][:, low:low + HID]
            down_w = down_weight[section][low:low + HID, :]
            ahead_share = jnp.sum(jnp.where(ahead_routes[section] == expert, ahead_weights[section], 0.0), axis=1)
            ahead_expert = expert_forward(ahead_tokens[section], gate_w, up_w, down_w)
            layer_out = layer_out + ahead_share[:, None] * ahead_expert.astype(jnp.float32)
            back_share = jnp.sum(jnp.where(back_routes[section] == expert, back_weights[section], 0.0), axis=1)
            back_expert = expert_backward(back_tokens[section], back_grads[section], gate_w, up_w, down_w)
            input_grad = input_grad + back_share[:, None] * back_expert.astype(jnp.float32)
        layer_list.append(layer_out.astype(jnp.bfloat16))
        grad_list.append(input_grad.astype(jnp.bfloat16))
    layers = jnp.stack(layer_list)
    grads = jnp.stack(grad_list)
    return jnp.roll(layers, 1, axis=0), jnp.roll(grads, -1, axis=0)
```

```python
import jax
import jax.numpy as jnp
from jax import lax
from jax.experimental import pallas as pl
from jax.experimental.pallas import tpu as pltpu
from jax.sharding import PartitionSpec as P

X, Z = 4, 8
Q = Z // 2
HOP = ((0, 0), (2, 6), (5, 1), (7, 3))
CAP = 10
CUTS = 4
CH = CAP * CUTS
LIMIT = 56 * 2**20
BF, F32 = jnp.bfloat16, jnp.float32


def along_z(k, back=False):
    pairs = []
    for x in range(X):
        for z in range(Z):
            a, b = x * Z + z, x * Z + (z + HOP[k][z % 2]) % Z
            pairs.append((b, a) if back else (a, b))
    return pairs


def along_x(dx):
    return [(x * Z + z, (x + dx) % X * Z + z) for x in range(X) for z in range(Z)]


def home(dx, step, sections):
    n = X * Z
    return [
        (s * n + x * Z + z, (s + step) % sections * n + (x - dx) % X * Z + z)
        for s in range(sections)
        for x in range(X)
        for z in range(Z)
    ]


def dot(a, b, dims=((1,), (0,))):
    return lax.dot_general(a, b, (dims, ((), ())), preferred_element_type=F32)


def call(kernel, outs, args, flops=0, scratch=(), hbm=(), after=()):
    moved = sum(a.size * a.dtype.itemsize for a in args) + sum(
        o.size * o.dtype.itemsize for o in outs
    )
    n = len(args)
    specs = [pl.BlockSpec(memory_space=pl.ANY if i in hbm else pltpu.VMEM) for i in range(n)]
    specs += [pl.BlockSpec(memory_space=pl.ANY)] * len(after)
    return pl.pallas_call(
        lambda *refs: kernel(*refs[:n], *refs[n + len(after) :]),
        out_shape=outs,
        in_specs=specs,
        out_specs=[pl.BlockSpec(memory_space=pltpu.VMEM)] * len(outs),
        scratch_shapes=list(scratch),
        compiler_params=pltpu.CompilerParams(vmem_limit_bytes=LIMIT),
        cost_estimate=pl.CostEstimate(flops=flops, bytes_accessed=moved, transcendentals=0),
    )(*args, *after)


def places(routes):
    count = routes.shape[0]
    me = lax.axis_index("expert")
    x, z = me // Z, me % Z
    same = routes[:, None] == routes[None, :]
    ids = jnp.arange(count, dtype=jnp.int32)
    earlier = ids[None, :] < ids[:, None]
    slot = jnp.sum((same & earlier).astype(jnp.int32), axis=1)
    dx = (routes // Q - x + X) % X
    dq = (routes % Q - z // 2 + Q) % Q
    odd = jnp.where(dq == 0, 0, dq % (Q - 1) + 1)
    k = jnp.where(z % 2 == 0, dq, odd)
    return (k * X + dx) * CH + slot


def pack_kernel(units, tgt, *refs):
    tokens, outs = refs[:units], refs[units:]
    rows = len(HOP) * X * CH
    count, width = tokens[0].shape[1:]
    cut = width // CUTS
    at = lax.broadcasted_iota(jnp.int32, (rows, count), 0)
    t = tgt[...]
    pick = jnp.concatenate(
        [(at == t + cb * CAP).astype(F32).astype(BF) for cb in range(CUTS)], axis=1
    )
    for u, ref in enumerate(tokens):
        v = ref[0]
        stacked = jnp.concatenate([v[:, cb * cut : (cb + 1) * cut] for cb in range(CUTS)], axis=0)
        got = dot(pick, stacked).astype(BF)
        part = rows // len(outs)
        for k, out in enumerate(outs):
            out[u * part : (u + 1) * part, :] = got[k * part : (k + 1) * part]


def pack(tgt, tokens, after):
    count, width = tokens[0].shape[1:]
    units, cut = len(tokens), width // CUTS
    rows = len(HOP) * X * CH
    outs = [jax.ShapeDtypeStruct((units * X * CH, cut), BF)] * len(HOP)
    return call(
        lambda *r: pack_kernel(units, *r),
        outs,
        (tgt[None, :], *tokens),
        flops=2 * units * rows * count * CUTS * cut,
        after=after,
    )


def regroup_kernel(*refs):
    half = len(refs) // 2
    ins, outs = refs[:half], refs[half:]
    part = half * CH
    for u in range(ins[0].shape[0] // part):
        for j in range(half):
            for i in range(half):
                outs[j][u * part + i * CH : u * part + (i + 1) * CH, :] = ins[i][
                    u * part + j * CH : u * part + (j + 1) * CH, :
                ]


def regroup(arrays, after=()):
    outs = [jax.ShapeDtypeStruct(a.shape, a.dtype) for a in arrays]
    return call(regroup_kernel, outs, arrays, after=after)


def shuffle(rows, back):
    shape = (rows, rows)
    plain = lax.broadcasted_iota(jnp.int32, shape, 1 if back else 0)
    packed = lax.broadcasted_iota(jnp.int32, shape, 0 if back else 1)
    per = rows // CUTS
    block = plain // per
    chunk = (plain % per) // CAP
    slot = plain % CAP
    return (packed == chunk * CH + block * CAP + slot).astype(F32).astype(BF)


def depack_kernel(*refs):
    ins, out = refs[:-1], refs[-1]
    part = len(ins) * CH
    rows = len(ins) * part
    per, cut = rows // CUTS, ins[0].shape[1]
    one = shuffle(rows, False)
    for u in range(ins[0].shape[0] // part):
        packed = jnp.concatenate([r[u * part : (u + 1) * part, :] for r in ins], axis=0)
        got = dot(one, packed).astype(BF)
        for cb in range(CUTS):
            out[u * per : (u + 1) * per, cb * cut : (cb + 1) * cut] = got[cb * per : (cb + 1) * per]


def depack(arrays):
    rows, cut = arrays[0].shape
    out = jax.ShapeDtypeStruct((len(arrays) * rows // CUTS, CUTS * cut), BF)
    n = len(arrays) * len(HOP) * CH
    return call(depack_kernel, [out], arrays, flops=2 * n * len(arrays) * rows * cut)[0]


def fetch(weights, bufs, sems):
    copies = [pltpu.make_async_copy(w.at[0], b, sems.at[i]) for i, (w, b) in enumerate(zip(weights, bufs))]
    for c in copies:
        c.start()
    return copies


def forward_kernel(own, other, *refs):
    weights, (mine, theirs), bufs, sems = refs[:6], refs[6:8], refs[8:14], refs[14]
    copies = fetch(weights, bufs, sems)
    rows, width = own.shape
    x = jnp.concatenate([own[...], other[...]], axis=0)
    hidden = []
    for h in range(2):
        copies[h].wait()
        gate = dot(x, bufs[h][...])
        copies[2 + h].wait()
        up = dot(x, bufs[2 + h][...])
        hidden.append((gate * jax.nn.sigmoid(gate) * up).astype(BF))
    copies[4].wait()
    copies[5].wait()
    cut = width // CUTS
    for cb in range(CUTS):
        cols = slice(cb * cut, (cb + 1) * cut)
        part = dot(hidden[0], bufs[4][:, cols]) + dot(hidden[1], bufs[5][:, cols])
        mine[:, cols] = part[:rows]
        theirs[:, cols] = part[rows:].astype(BF)


def backward_kernel(own, other, *refs):
    weights, (mine, theirs), bufs, sems = refs[:6], refs[6:8], refs[8:14], refs[14]
    copies = fetch(weights, bufs, sems)
    rows, width = own.shape[0] // 2, own.shape[1]
    x = jnp.concatenate([own[:rows, :], other[:rows, :]], axis=0)
    g = jnp.concatenate([own[rows:, :], other[rows:, :]], axis=0)
    back = []
    for h in range(2):
        copies[h].wait()
        gate = dot(x, bufs[h][...])
        copies[2 + h].wait()
        up = dot(x, bufs[2 + h][...])
        copies[4 + h].wait()
        carried = dot(g, bufs[4 + h][...], ((1,), (1,)))
        sigma = jax.nn.sigmoid(gate)
        d_gate = (carried * up * sigma * (1.0 + gate * (1.0 - sigma))).astype(BF)
        d_up = (carried * gate * sigma).astype(BF)
        back.append((d_gate, d_up))
    cut = width // CUTS
    for cb in range(CUTS):
        cols = slice(cb * cut, (cb + 1) * cut)
        part = None
        for h in range(2):
            for i in range(2):
                term = dot(back[h][i], bufs[2 * i + h][cols, :], ((1,), (1,)))
                part = term if part is None else part + term
        mine[:, cols] = part[:rows]
        theirs[:, cols] = part[rows:].astype(BF)


def experts(kernel, own, other, weights, rows, products):
    width = own.shape[1]
    outs = [jax.ShapeDtypeStruct((rows, width), F32), jax.ShapeDtypeStruct((rows, width), BF)]
    scratch = [pltpu.VMEM(w.shape[1:], BF) for w in weights] + [pltpu.SemaphoreType.DMA((6,))]
    hid = 2 * weights[0].shape[2]
    return call(
        kernel,
        outs,
        (own, other, *weights),
        flops=2 * products * 2 * rows * width * hid,
        scratch=scratch,
        hbm=range(2, 8),
    )


def add_kernel(mine, got, *outs):
    rows, width = mine.shape
    cut = width // CUTS
    total = (mine[...] + got[...].astype(F32)).astype(BF)
    stacked = jnp.concatenate([total[:, cb * cut : (cb + 1) * cut] for cb in range(CUTS)], axis=0)
    packed = dot(shuffle(rows * CUTS, True), stacked).astype(BF)
    part = rows * CUTS // len(outs)
    for i, out in enumerate(outs):
        out[...] = packed[i * part : (i + 1) * part]


def add(mine, got):
    rows, width = mine.shape
    outs = [jax.ShapeDtypeStruct((rows * CUTS // X, width // CUTS), BF)] * X
    return call(add_kernel, outs, (mine, got), flops=2 * (rows * CUTS) ** 2 * width // CUTS)


def unpack_kernel(tgt, mix, *refs):
    ins, out = refs[:-1], refs[-1]
    packed = jnp.concatenate([r[...] for r in ins], axis=0)
    rows, cut = packed.shape
    count = tgt.shape[0]
    at = lax.broadcasted_iota(jnp.int32, (count, rows), 1)
    t, w = tgt[...], mix[...]
    for cb in range(CUTS):
        pick = (at == t + cb * CAP).astype(F32).astype(BF)
        out[0, :, cb * cut : (cb + 1) * cut] = (dot(pick, packed) * w).astype(BF)


def unpack(tgt, mix, arrays):
    rows, cut = arrays[0].shape
    count = tgt.shape[0]
    out = jax.ShapeDtypeStruct((1, count, CUTS * cut), BF)
    return call(
        unpack_kernel,
        [out],
        (tgt, mix, *arrays),
        flops=2 * CUTS * count * len(arrays) * rows * cut,
    )[0]


def send_along_z(chunks, back=False):
    return [chunks[0]] + [
        lax.ppermute(chunks[k], "expert", along_z(k, back)) for k in range(1, len(HOP))
    ]


def send_along_x(columns):
    return [columns[0]] + [
        lax.ppermute(columns[dx], "expert", along_x(dx)) for dx in range(1, X)
    ]


def to_pair(rows):
    return lax.ppermute(rows, "expert", [(i, i ^ 1) for i in range(X * Z)])


def collect(mine, theirs, step):
    sections = lax.axis_size("section")
    columns = add(mine, to_pair(theirs))
    columns = [
        lax.ppermute(columns[dx], ("section", "expert"), home(dx, step, sections)) for dx in range(X)
    ]
    return send_along_z(regroup(columns), True)


def table(tgt, weights, step):
    count = lax.axis_size("section")
    both = jnp.stack([tgt.astype(F32), weights])
    both = lax.ppermute(both, "section", [(i, (i + step) % count) for i in range(count)])
    return both[0].astype(jnp.int32)[:, None], both[1][:, None]


def on_device(
    ahead_tokens,
    ahead_routes,
    ahead_weights,
    back_tokens,
    back_grads,
    back_routes,
    back_weights,
    gate_weight,
    up_weight,
    down_weight,
):
    def to_narrow(w, *before):
        if before:
            w = lax.optimization_barrier((w, *before))[0]
        return lax.ppermute(w, "narrow", [(0, 1), (1, 0)])

    ahead_tgt = places(ahead_routes[0, :, 0])
    back_tgt = places(back_routes[0, :, 0])
    gate_other = to_narrow(gate_weight)
    ahead_chunks = pack(ahead_tgt, [ahead_tokens], [])
    back_chunks = pack(back_tgt, [back_tokens, back_grads], [ahead_chunks[0]])
    ahead_chunks = send_along_z(ahead_chunks)
    ahead_columns = regroup(ahead_chunks, [gate_other, back_chunks[0]])
    up_other = to_narrow(up_weight, ahead_columns[0])
    back_chunks = send_along_z(back_chunks)
    ahead_own = depack(send_along_x(ahead_columns))
    ahead_other = to_pair(ahead_own)
    back_columns = regroup(back_chunks, [ahead_own, up_other])
    down_other = to_narrow(down_weight, back_columns[0])
    back_own = depack(send_along_x(back_columns))
    back_other = to_pair(back_own)
    weights = [gate_weight, gate_other, up_weight, up_other, down_weight, down_other]
    ahead_table = table(ahead_tgt, ahead_weights[0, :, 0], 1)
    back_table = table(back_tgt, back_weights[0, :, 0], -1)
    rows = X * len(HOP) * CAP
    mine, theirs = experts(forward_kernel, ahead_own, ahead_other, weights, rows, 3)
    ahead_chunks = collect(mine, theirs, 1)
    mine, theirs = experts(backward_kernel, back_own, back_other, weights, rows, 5)
    back_chunks = collect(mine, theirs, -1)
    return unpack(*ahead_table, ahead_chunks), unpack(*back_table, back_chunks)


def solution(mesh):
    tokens = P("section", ("expert", "narrow"), None)
    columns = P("section", None, ("expert", "narrow"))
    in_specs = (tokens,) * 7 + (columns, columns, tokens)
    return jax.shard_map(
        on_device, mesh=mesh, in_specs=in_specs, out_specs=(tokens, tokens), check_vma=False
    )
```

```python
import jax
import jax.numpy as jnp
from jax import lax
from jax.experimental import pallas as pl
from jax.experimental.pallas import tpu as pltpu
from jax.sharding import Mesh
from jax.sharding import PartitionSpec as P

X, Z = 4, 8
Q = Z // 2
HOP = ((0, 0), (2, 6), (5, 1), (7, 3))
CAP = 10
CUTS = 4
CH = CAP * CUTS
LIMIT = 56 * 2**20
BF, F32 = jnp.bfloat16, jnp.float32


def along_z(k):
    return [
        (x * Z + z, x * Z + (z + HOP[k][z % 2]) % Z) for x in range(X) for z in range(Z)
    ]


def home(k, step, sections):
    n = X * Z
    return [
        (s * n + b, (s + step) % sections * n + a) for s in range(sections) for a, b in along_z(k)
    ]


def dot(a, b, dims=((1,), (0,))):
    return lax.dot_general(a, b, (dims, ((), ())), preferred_element_type=F32)


def call(kernel, outs, args, flops=0, scratch=(), hbm=(), after=()):
    moved = sum(a.size * a.dtype.itemsize for a in args) + sum(
        o.size * o.dtype.itemsize for o in outs
    )
    n = len(args)
    specs = [pl.BlockSpec(memory_space=pl.ANY if i in hbm else pltpu.VMEM) for i in range(n)]
    specs += [pl.BlockSpec(memory_space=pl.ANY)] * len(after)
    return pl.pallas_call(
        lambda *refs: kernel(*refs[:n], *refs[n + len(after) :]),
        out_shape=outs,
        in_specs=specs,
        out_specs=[pl.BlockSpec(memory_space=pltpu.VMEM)] * len(outs),
        scratch_shapes=list(scratch),
        compiler_params=pltpu.CompilerParams(vmem_limit_bytes=LIMIT),
        cost_estimate=pl.CostEstimate(flops=flops, bytes_accessed=moved, transcendentals=0),
    )(*args, *after)


def places(routes):
    count = routes.shape[0]
    z = lax.axis_index("z")
    same = routes[:, None] == routes[None, :]
    ids = jnp.arange(count, dtype=jnp.int32)
    earlier = ids[None, :] < ids[:, None]
    slot = jnp.sum((same & earlier).astype(jnp.int32), axis=1)
    dq = (routes % Q - z // 2 + Q) % Q
    odd = jnp.where(dq == 0, 0, dq % (Q - 1) + 1)
    k = jnp.where(z % 2 == 0, dq, odd)
    return (k * X + routes // Q) * CH + slot


def pack_kernel(units, tgt, *refs):
    tokens, outs = refs[:units], refs[units:]
    rows = len(HOP) * X * CH
    count, width = tokens[0].shape[1:]
    cut, part = width // CUTS, rows // len(HOP)
    at = lax.broadcasted_iota(jnp.int32, (rows, count), 0)
    t = tgt[...]
    pick = jnp.concatenate(
        [(at == t + cb * CAP).astype(F32).astype(BF) for cb in range(CUTS)], axis=1
    )
    for u, ref in enumerate(tokens):
        v = ref[0]
        stacked = jnp.concatenate([v[:, cb * cut : (cb + 1) * cut] for cb in range(CUTS)], axis=0)
        got = dot(pick, stacked).astype(BF)
        for k in range(len(HOP)):
            outs[u * len(HOP) + k][...] = got[k * part : (k + 1) * part]


def pack(tgt, tokens, after=()):
    count, width = tokens[0].shape[1:]
    units, cut = len(tokens), width // CUTS
    rows = len(HOP) * X * CH
    outs = [jax.ShapeDtypeStruct((X * CH, cut), BF)] * (units * len(HOP))
    got = call(
        lambda *r: pack_kernel(units, *r),
        outs,
        (tgt[None, :], *tokens),
        flops=2 * units * rows * count * CUTS * cut,
        after=after,
    )
    return [got[u * len(HOP) : (u + 1) * len(HOP)] for u in range(units)]


def by_column_kernel(*refs):
    ins, out = refs[:-1], refs[-1]
    for x in range(X):
        for k, r in enumerate(ins):
            out[x, k * CH : (k + 1) * CH, :] = r[x * CH : (x + 1) * CH, :]


def by_column(chunks, after=()):
    out = jax.ShapeDtypeStruct((X, len(chunks) * CH, chunks[0].shape[1]), BF)
    return call(by_column_kernel, [out], chunks, after=after)[0]


def by_route_kernel(columns, *outs):
    for k, out in enumerate(outs):
        for x in range(X):
            out[x * CH : (x + 1) * CH, :] = columns[x, k * CH : (k + 1) * CH, :]


def by_route(columns, after=()):
    outs = [jax.ShapeDtypeStruct((X * CH, columns.shape[2]), BF)] * len(HOP)
    return call(by_route_kernel, outs, (columns,), after=after)


def shuffle(rows, back):
    shape = (rows, rows)
    plain = lax.broadcasted_iota(jnp.int32, shape, 1 if back else 0)
    packed = lax.broadcasted_iota(jnp.int32, shape, 0 if back else 1)
    per = rows // CUTS
    block = plain // per
    chunk = (plain % per) // CAP
    slot = plain % CAP
    return (packed == chunk * CH + block * CAP + slot).astype(F32).astype(BF)


def depack_kernel(columns, out):
    n, part, cut = columns.shape
    rows, per = n * part, n * part // CUTS
    packed = jnp.concatenate([columns[i] for i in range(n)], axis=0)
    got = dot(shuffle(rows, False), packed).astype(BF)
    for cb in range(CUTS):
        out[:, cb * cut : (cb + 1) * cut] = got[cb * per : (cb + 1) * per]


def depack(columns, after=()):
    n, part, cut = columns.shape
    out = jax.ShapeDtypeStruct((n * part // CUTS, CUTS * cut), BF)
    return call(depack_kernel, [out], (columns,), flops=2 * (n * part) ** 2 * cut, after=after)[0]


def fetch(weights, bufs, sems):
    copies = [pltpu.make_async_copy(w.at[0], b, sems.at[i]) for i, (w, b) in enumerate(zip(weights, bufs))]
    for c in copies:
        c.start()
    return copies


def forward_kernel(own, other, *refs):
    weights, (mine, theirs), bufs, sems = refs[:6], refs[6:8], refs[8:14], refs[14]
    copies = fetch(weights, bufs, sems)
    rows, width = own.shape
    x = jnp.concatenate([own[...], other[...]], axis=0)
    hidden = []
    for h in range(2):
        copies[h].wait()
        gate = dot(x, bufs[h][...])
        copies[2 + h].wait()
        up = dot(x, bufs[2 + h][...])
        hidden.append((gate * jax.nn.sigmoid(gate) * up).astype(BF))
    copies[4].wait()
    copies[5].wait()
    cut = width // CUTS
    for cb in range(CUTS):
        cols = slice(cb * cut, (cb + 1) * cut)
        part = dot(hidden[0], bufs[4][:, cols]) + dot(hidden[1], bufs[5][:, cols])
        mine[:, cols] = part[:rows]
        theirs[:, cols] = part[rows:].astype(BF)


def backward_kernel(x_own, x_other, g_own, g_other, *refs):
    weights, (mine, theirs), bufs, sems = refs[:6], refs[6:8], refs[8:14], refs[14]
    copies = fetch(weights, bufs, sems)
    rows, width = x_own.shape
    x = jnp.concatenate([x_own[...], x_other[...]], axis=0)
    g = jnp.concatenate([g_own[...], g_other[...]], axis=0)
    back = []
    for h in range(2):
        copies[h].wait()
        gate = dot(x, bufs[h][...])
        copies[2 + h].wait()
        up = dot(x, bufs[2 + h][...])
        copies[4 + h].wait()
        carried = dot(g, bufs[4 + h][...], ((1,), (1,)))
        sigma = jax.nn.sigmoid(gate)
        d_gate = (carried * up * sigma * (1.0 + gate * (1.0 - sigma))).astype(BF)
        d_up = (carried * gate * sigma).astype(BF)
        back.append((d_gate, d_up))
    cut = width // CUTS
    for cb in range(CUTS):
        cols = slice(cb * cut, (cb + 1) * cut)
        part = None
        for h in range(2):
            for i in range(2):
                term = dot(back[h][i], bufs[2 * i + h][cols, :], ((1,), (1,)))
                part = term if part is None else part + term
        mine[:, cols] = part[:rows]
        theirs[:, cols] = part[rows:].astype(BF)


def experts(kernel, rows, weights, products, after=()):
    count, width = rows[0].shape
    outs = [jax.ShapeDtypeStruct((count, width), F32), jax.ShapeDtypeStruct((count, width), BF)]
    scratch = [pltpu.VMEM(w.shape[1:], BF) for w in weights] + [pltpu.SemaphoreType.DMA((6,))]
    hid = 2 * weights[0].shape[2]
    n = len(rows)
    return call(
        kernel,
        outs,
        (*rows, *weights),
        flops=2 * products * 2 * count * width * hid,
        scratch=scratch,
        hbm=range(n, n + 6),
        after=after,
    )


def add_kernel(mine, got, out):
    rows, width = mine.shape
    cut = width // CUTS
    total = (mine[...] + got[...].astype(F32)).astype(BF)
    stacked = jnp.concatenate([total[:, cb * cut : (cb + 1) * cut] for cb in range(CUTS)], axis=0)
    packed = dot(shuffle(rows * CUTS, True), stacked).astype(BF)
    part = rows * CUTS // X
    for x in range(X):
        out[x] = packed[x * part : (x + 1) * part]


def add(mine, got, after=()):
    rows, width = mine.shape
    out = jax.ShapeDtypeStruct((X, rows * CUTS // X, width // CUTS), BF)
    flops = 2 * (rows * CUTS) ** 2 * width // CUTS
    return call(add_kernel, [out], (mine, got), flops=flops, after=after)[0]


def unpack_kernel(tgt, mix, *refs):
    ins, out = refs[:-1], refs[-1]
    packed = jnp.concatenate([r[...] for r in ins], axis=0)
    rows, cut = packed.shape
    count = tgt.shape[0]
    at = lax.broadcasted_iota(jnp.int32, (count, rows), 1)
    t, w = tgt[...], mix[...]
    for cb in range(CUTS):
        pick = (at == t + cb * CAP).astype(F32).astype(BF)
        out[0, :, cb * cut : (cb + 1) * cut] = (dot(pick, packed) * w).astype(BF)


def unpack(tgt, mix, arrays):
    rows, cut = arrays[0].shape
    count = tgt.shape[0]
    out = jax.ShapeDtypeStruct((1, count, CUTS * cut), BF)
    return call(
        unpack_kernel,
        [out],
        (tgt, mix, *arrays),
        flops=2 * CUTS * count * len(arrays) * rows * cut,
    )[0]


def send(chunks):
    return [chunks[0]] + [
        lax.ppermute(chunks[k], ("x", "z"), along_z(k)) for k in range(1, len(HOP))
    ]


def across(columns):
    return lax.all_to_all(columns, "x", 0, 0, tiled=True)


def to_pair(rows):
    return lax.ppermute(rows, "z", [(z, z ^ 1) for z in range(Z)])


def to_narrow(w):
    return lax.ppermute(w, "narrow", [(0, 1), (1, 0)])


def held(array, *before):
    return lax.optimization_barrier((array, *before))[0]


def send_home(chunks, step):
    sections = lax.axis_size("section")
    return [
        lax.ppermute(chunks[k], ("section", "x", "z"), home(k, step, sections))
        for k in range(len(HOP))
    ]


def table(tgt, weights, step):
    count = lax.axis_size("section")
    both = jnp.stack([tgt.astype(F32), weights])
    both = lax.ppermute(both, "section", [(i, (i + step) % count) for i in range(count)])
    return both[0].astype(jnp.int32)[:, None], both[1][:, None]


def on_device(
    ahead_tokens,
    ahead_routes,
    ahead_weights,
    back_tokens,
    back_grads,
    back_routes,
    back_weights,
    gate_weight,
    up_weight,
    down_weight,
):
    ahead_tgt = places(ahead_routes[0, :, 0])
    back_tgt = places(back_routes[0, :, 0])
    gate_other = to_narrow(gate_weight)
    (ahead,) = pack(ahead_tgt, [ahead_tokens])
    back, grad = pack(back_tgt, [back_tokens, back_grads], [ahead[0]])
    ahead_table = table(ahead_tgt, ahead_weights[0, :, 0], 1)
    back_table = table(back_tgt, back_weights[0, :, 0], -1)

    ahead = by_column(send(ahead), [gate_other, back[0]])
    up_other = to_narrow(held(up_weight, ahead))
    back = send([back[0]] + [held(c, ahead) for c in back[1:]])
    ahead_own = depack(across(ahead))
    ahead_other = to_pair(ahead_own)

    back = by_column(back, [up_other, ahead_own])
    down_other = to_narrow(held(down_weight, back))
    grad = send([grad[0]] + [held(c, back) for c in grad[1:]])
    back_own = depack(across(back), [ahead_other])
    back_other = to_pair(back_own)

    grad = by_column(grad, [back_own, *ahead_table, *back_table])
    grad_own = depack(across(grad), [back_other])
    grad_other = to_pair(grad_own)

    weights = [gate_weight, gate_other, up_weight, up_other, down_weight, down_other]
    mine, theirs = experts(forward_kernel, [ahead_own, ahead_other], weights, 3, [grad_own])
    ahead_sum = add(mine, to_pair(theirs))
    rows = [back_own, back_other, grad_own, grad_other]
    mine, theirs = experts(backward_kernel, rows, weights, 5, [theirs])
    ahead = by_route(across(ahead_sum), [theirs])
    back_sum = add(mine, to_pair(theirs), [ahead[0]])
    ahead = send_home(ahead, 1)
    back = send_home(by_route(across(back_sum)), -1)
    return unpack(*ahead_table, ahead), unpack(*back_table, back)


def solution(mesh):
    grid = Mesh(
        mesh.devices.reshape(mesh.shape["section"], X, Z, mesh.shape["narrow"]),
        ("section", "x", "z", "narrow"),
    )
    split = ("x", "z", "narrow")
    tokens = P("section", split, None)
    columns = P("section", None, split)
    in_specs = (tokens,) * 7 + (columns, columns, tokens)
    return jax.shard_map(
        on_device, mesh=grid, in_specs=in_specs, out_specs=(tokens, tokens), check_vma=False
    )
```

```python
import jax
import jax.numpy as jnp
from jax import lax
from jax.experimental import pallas as pl
from jax.experimental.pallas import tpu as pltpu
from jax.sharding import Mesh
from jax.sharding import PartitionSpec as P

X, Z = 4, 8
Q = Z // 2
HOP = ((0, 0), (2, 6), (5, 1), (7, 3))
CAP = 10
CUTS = 4
CH = CAP * CUTS
LIMIT = 56 * 2**20
BF, F32 = jnp.bfloat16, jnp.float32


def along_z(k):
    return [
        (x * Z + z, x * Z + (z + HOP[k][z % 2]) % Z) for x in range(X) for z in range(Z)
    ]


def home(k, step, sections):
    n = X * Z
    return [
        (s * n + b, (s + step) % sections * n + a) for s in range(sections) for a, b in along_z(k)
    ]


def dot(a, b, dims=((1,), (0,))):
    return lax.dot_general(a, b, (dims, ((), ())), preferred_element_type=F32)


def call(kernel, outs, args, flops=0, scratch=(), hbm=(), after=()):
    moved = sum(a.size * a.dtype.itemsize for a in args) + sum(
        o.size * o.dtype.itemsize for o in outs
    )
    n = len(args)
    specs = [pl.BlockSpec(memory_space=pl.ANY if i in hbm else pltpu.VMEM) for i in range(n)]
    specs += [pl.BlockSpec(memory_space=pl.ANY)] * len(after)
    return pl.pallas_call(
        lambda *refs: kernel(*refs[:n], *refs[n + len(after) :]),
        out_shape=outs,
        in_specs=specs,
        out_specs=[pl.BlockSpec(memory_space=pltpu.VMEM)] * len(outs),
        scratch_shapes=list(scratch),
        compiler_params=pltpu.CompilerParams(vmem_limit_bytes=LIMIT),
        cost_estimate=pl.CostEstimate(flops=flops, bytes_accessed=moved, transcendentals=0),
    )(*args, *after)


def places(routes):
    count = routes.shape[0]
    z = lax.axis_index("z")
    same = routes[:, None] == routes[None, :]
    ids = jnp.arange(count, dtype=jnp.int32)
    earlier = ids[None, :] < ids[:, None]
    slot = jnp.sum((same & earlier).astype(jnp.int32), axis=1)
    dq = (routes % Q - z // 2 + Q) % Q
    odd = jnp.where(dq == 0, 0, dq % (Q - 1) + 1)
    k = jnp.where(z % 2 == 0, dq, odd)
    return (k * X + routes // Q) * CH + slot


def pack_kernel(units, tgt, *refs):
    tokens, outs = refs[:units], refs[units:]
    rows = len(HOP) * X * CH
    count, width = tokens[0].shape[1:]
    cut, part = width // CUTS, rows // len(HOP)
    at = lax.broadcasted_iota(jnp.int32, (rows, count), 0)
    t = tgt[...]
    pick = jnp.concatenate(
        [(at == t + cb * CAP).astype(F32).astype(BF) for cb in range(CUTS)], axis=1
    )
    for u, ref in enumerate(tokens):
        v = ref[0]
        stacked = jnp.concatenate([v[:, cb * cut : (cb + 1) * cut] for cb in range(CUTS)], axis=0)
        got = dot(pick, stacked).astype(BF)
        for k in range(len(HOP)):
            outs[u * len(HOP) + k][...] = got[k * part : (k + 1) * part]


def pack(tgt, tokens, after=()):
    count, width = tokens[0].shape[1:]
    units, cut = len(tokens), width // CUTS
    rows = len(HOP) * X * CH
    outs = [jax.ShapeDtypeStruct((X * CH, cut), BF)] * (units * len(HOP))
    got = call(
        lambda *r: pack_kernel(units, *r),
        outs,
        (tgt[None, :], *tokens),
        flops=2 * units * rows * count * CUTS * cut,
        after=after,
    )
    return [got[u * len(HOP) : (u + 1) * len(HOP)] for u in range(units)]


def by_column_kernel(*refs):
    ins, out = refs[:-1], refs[-1]
    for x in range(X):
        for k, r in enumerate(ins):
            out[x, k * CH : (k + 1) * CH, :] = r[x * CH : (x + 1) * CH, :]


def by_column(chunks, after=()):
    out = jax.ShapeDtypeStruct((X, len(chunks) * CH, chunks[0].shape[1]), BF)
    return call(by_column_kernel, [out], chunks, after=after)[0]


def by_route_kernel(columns, *outs):
    for k, out in enumerate(outs):
        for x in range(X):
            out[x * CH : (x + 1) * CH, :] = columns[x, k * CH : (k + 1) * CH, :]


def by_route(columns, after=()):
    outs = [jax.ShapeDtypeStruct((X * CH, columns.shape[2]), BF)] * len(HOP)
    return call(by_route_kernel, outs, (columns,), after=after)


def shuffle(rows, back):
    shape = (rows, rows)
    plain = lax.broadcasted_iota(jnp.int32, shape, 1 if back else 0)
    packed = lax.broadcasted_iota(jnp.int32, shape, 0 if back else 1)
    per = rows // CUTS
    block = plain // per
    chunk = (plain % per) // CAP
    slot = plain % CAP
    return (packed == chunk * CH + block * CAP + slot).astype(F32).astype(BF)


def depack_kernel(columns, out):
    cut = columns.shape[2]
    for cb, part in enumerate(plain(columns)):
        out[:, cb * cut : (cb + 1) * cut] = part


def depack(columns, after=()):
    n, part, cut = columns.shape
    out = jax.ShapeDtypeStruct((n * part // CUTS, CUTS * cut), BF)
    return call(depack_kernel, [out], (columns,), flops=2 * (n * part) ** 2 * cut, after=after)[0]


def fetch(weights, bufs, sems):
    copies = [
        pltpu.make_async_copy(w.at[0], b, sems.at[i]) for i, (w, b) in enumerate(zip(weights, bufs))
    ]
    for c in copies:
        c.start()
    return copies


def plain(columns):
    n, part, _ = columns.shape
    packed = jnp.concatenate([columns[i] for i in range(n)], axis=0)
    got = dot(shuffle(n * part, False), packed).astype(BF)
    per = n * part // CUTS
    return [got[cb * per : (cb + 1) * per] for cb in range(CUTS)]


def to_columns(total, out):
    stacked = jnp.concatenate(total, axis=0)
    rows = stacked.shape[0]
    packed = dot(shuffle(rows, True), stacked).astype(BF)
    part = rows // X
    for x in range(X):
        out[x] = packed[x * part : (x + 1) * part]


def hidden_kernel(own, other, *refs):
    weights, (mine, theirs), bufs, sems = refs[:4], refs[4:6], refs[6:10], refs[10]
    copies = fetch(weights, bufs, sems)
    rows = own.shape[0]
    x = jnp.concatenate([own[...], other[...]], axis=0)
    hid = bufs[0].shape[1]
    for h in range(2):
        cols = slice(h * hid, (h + 1) * hid)
        copies[h].wait()
        gate = dot(x, bufs[h][...])
        copies[2 + h].wait()
        up = dot(x, bufs[2 + h][...])
        hidden = (gate * jax.nn.sigmoid(gate) * up).astype(BF)
        mine[:, cols] = hidden[:rows]
        theirs[:, cols] = hidden[rows:]


def down_kernel(own, other, *refs):
    weights, out, bufs, sems = refs[:4], refs[4], refs[5:9], refs[9]
    copies = fetch(weights, bufs, sems)
    hid, width = bufs[0].shape
    cut = width // CUTS
    values = [own[:, :hid], own[:, hid:], other[:, :hid], other[:, hid:]]
    for c in copies:
        c.wait()
    total = []
    for cb in range(CUTS):
        part = None
        for h in range(4):
            term = dot(values[h], bufs[h][:, cb * cut : (cb + 1) * cut])
            part = term if part is None else part + term
        total.append(part.astype(BF))
    to_columns(total, out)


def carried_kernel(columns, *refs):
    weights, (mine, theirs), bufs, sems = refs[:4], refs[4:6], refs[6:10], refs[10]
    copies = fetch(weights, bufs, sems)
    hid = bufs[0].shape[0]
    g = jnp.concatenate(plain(columns), axis=1)
    for h, out in enumerate((mine, mine, theirs, theirs)):
        copies[h].wait()
        cols = slice(h % 2 * hid, (h % 2 + 1) * hid)
        out[:, cols] = dot(g, bufs[h][...], ((1,), (1,)))


def backward_kernel(own, other, c_own, c_other, *refs):
    weights, (mine, theirs), bufs, sems = refs[:4], refs[4:6], refs[6:10], refs[10]
    copies = fetch(weights, bufs, sems)
    rows, width = own.shape
    hid = bufs[0].shape[1]
    x = jnp.concatenate([own[...], other[...]], axis=0)
    back = []
    for h in range(2):
        cols = slice(h * hid, (h + 1) * hid)
        copies[h].wait()
        gate = dot(x, bufs[h][...])
        copies[2 + h].wait()
        up = dot(x, bufs[2 + h][...])
        carried = jnp.concatenate([c_own[:, cols], c_other[:, cols]], axis=0)
        sigma = jax.nn.sigmoid(gate)
        d_gate = (carried * up * sigma * (1.0 + gate * (1.0 - sigma))).astype(BF)
        d_up = (carried * gate * sigma).astype(BF)
        back.append((d_gate, d_up))
    cut = width // CUTS
    for cb in range(CUTS):
        cols = slice(cb * cut, (cb + 1) * cut)
        part = None
        for h in range(2):
            for i in range(2):
                term = dot(back[h][i], bufs[2 * i + h][cols, :], ((1,), (1,)))
                part = term if part is None else part + term
        mine[:, cols] = part[:rows]
        theirs[:, cols] = part[rows:].astype(BF)


def experts(kernel, outs, rows, weights, products, after=()):
    scratch = [pltpu.VMEM(w.shape[1:], BF) for w in weights] + [pltpu.SemaphoreType.DMA((4,))]
    n = len(rows)
    return call(
        kernel,
        outs,
        (*rows, *weights),
        flops=2 * products * X * len(HOP) * CAP * 4 * weights[0].size,
        scratch=scratch,
        hbm=range(n, n + 4),
        after=after,
    )


def add_kernel(mine, got, out):
    cut = mine.shape[1] // CUTS
    total = (mine[...] + got[...].astype(F32)).astype(BF)
    to_columns([total[:, cb * cut : (cb + 1) * cut] for cb in range(CUTS)], out)


def add(mine, got, after=()):
    rows, width = mine.shape
    out = jax.ShapeDtypeStruct((X, rows * CUTS // X, width // CUTS), BF)
    flops = 2 * (rows * CUTS) ** 2 * width // CUTS
    return call(add_kernel, [out], (mine, got), flops=flops, after=after)[0]


def unpack_kernel(tgt, mix, *refs):
    ins, out = refs[:-1], refs[-1]
    packed = jnp.concatenate([r[...] for r in ins], axis=0)
    rows, cut = packed.shape
    count = tgt.shape[0]
    at = lax.broadcasted_iota(jnp.int32, (count, rows), 1)
    t, w = tgt[...], mix[...]
    for cb in range(CUTS):
        pick = (at == t + cb * CAP).astype(F32).astype(BF)
        out[0, :, cb * cut : (cb + 1) * cut] = (dot(pick, packed) * w).astype(BF)


def unpack(tgt, mix, arrays):
    rows, cut = arrays[0].shape
    count = tgt.shape[0]
    out = jax.ShapeDtypeStruct((1, count, CUTS * cut), BF)
    return call(
        unpack_kernel,
        [out],
        (tgt, mix, *arrays),
        flops=2 * CUTS * count * len(arrays) * rows * cut,
    )[0]


def send(chunks):
    return [chunks[0]] + [
        lax.ppermute(chunks[k], ("x", "z"), along_z(k)) for k in range(1, len(HOP))
    ]


def across(columns):
    return lax.all_to_all(columns, "x", 0, 0, tiled=True)


def to_pair(rows):
    return lax.ppermute(rows, "z", [(z, z ^ 1) for z in range(Z)])


def to_narrow(w):
    return lax.ppermute(w, "narrow", [(0, 1), (1, 0)])


def held(array, *before):
    return lax.optimization_barrier((array, *before))[0]


def send_home(chunks, step):
    sections = lax.axis_size("section")
    return [
        lax.ppermute(chunks[k], ("section", "x", "z"), home(k, step, sections))
        for k in range(len(HOP))
    ]


def table(tgt, weights, step):
    count = lax.axis_size("section")
    both = jnp.stack([tgt.astype(F32), weights])
    both = lax.ppermute(both, "section", [(i, (i + step) % count) for i in range(count)])
    return both[0].astype(jnp.int32)[:, None], both[1][:, None]


def on_device(
    ahead_tokens,
    ahead_routes,
    ahead_weights,
    back_tokens,
    back_grads,
    back_routes,
    back_weights,
    gate_weight,
    up_weight,
    down_weight,
):
    ahead_tgt = places(ahead_routes[0, :, 0])
    back_tgt = places(back_routes[0, :, 0])
    down_1 = to_narrow(down_weight)
    down_2 = to_pair(down_weight)
    (ahead,) = pack(ahead_tgt, [ahead_tokens])
    back, grad = pack(back_tgt, [back_tokens, back_grads], [ahead[0]])
    ahead_table = table(ahead_tgt, ahead_weights[0, :, 0], 1)
    back_table = table(back_tgt, back_weights[0, :, 0], -1)

    ahead = send(ahead)
    back = send([back[0]] + [held(c, a) for c, a in zip(back[1:], ahead[1:])])
    ahead = by_column(ahead, [down_1, back[0]])
    down_3 = to_narrow(held(down_2, ahead))
    gate_1 = to_narrow(held(gate_weight, ahead))
    ahead_own = depack(across(ahead))
    ahead_other = to_pair(ahead_own)

    grad = send([grad[0]] + [held(c, b) for c, b in zip(grad[1:], back[1:])])
    back = by_column(back, [ahead_other, down_3, gate_1])
    up_1 = to_narrow(held(up_weight, back))
    back_own = depack(across(back))
    back_other = to_pair(back_own)
    grad = by_column(grad, [back, *ahead_table, *back_table])

    rows, width = ahead_own.shape
    hid = 2 * down_weight.shape[1]
    down = [down_weight, down_1, down_2, down_3]
    into = [gate_weight, gate_1, up_weight, up_1]
    outs = [jax.ShapeDtypeStruct((rows, hid), F32)] * 2
    c_own, c_send = experts(carried_kernel, outs, [across(grad)], down, 1, [back_own])
    c_other = to_pair(c_send)

    outs = [jax.ShapeDtypeStruct((rows, hid), BF)] * 2
    h_own, h_send = experts(hidden_kernel, outs, [ahead_own, ahead_other], into, 2, [c_own, back_other])
    h_other = to_pair(h_send)

    outs = [jax.ShapeDtypeStruct((rows, width), t) for t in (F32, BF)]
    inputs = [back_own, back_other, c_own, c_other]
    mine, theirs = experts(backward_kernel, outs, inputs, into, 4, [h_send])

    outs = [jax.ShapeDtypeStruct((X, rows * CUTS // X, width // CUTS), BF)]
    (ahead,) = experts(down_kernel, outs, [h_own, h_other], down, 1, [theirs])
    ahead = by_route(across(ahead))
    back = add(mine, to_pair(theirs), [ahead[0]])
    ahead = send_home(ahead, 1)
    back = send_home(by_route(across(back)), -1)
    return unpack(*ahead_table, ahead), unpack(*back_table, back)


def solution(mesh):
    grid = Mesh(
        mesh.devices.reshape(mesh.shape["section"], X, Z, mesh.shape["narrow"]),
        ("section", "x", "z", "narrow"),
    )
    split = ("x", "z", "narrow")
    tokens = P("section", split, None)
    columns = P("section", None, split)
    in_specs = (tokens,) * 7 + (columns, columns, tokens)
    return jax.shard_map(
        on_device, mesh=grid, in_specs=in_specs, out_specs=(tokens, tokens), check_vma=False
    )
```

```python
import jax
import jax.numpy as jnp
from jax import lax
from jax.experimental import pallas as pl
from jax.experimental.pallas import tpu as pltpu
from jax.sharding import Mesh
from jax.sharding import PartitionSpec as P

X, Z = 4, 8
Q = Z // 2
HOP = ((0, 0), (2, 6), (5, 1), (7, 3))
CAP = 10
CUTS = 4
CH = CAP * CUTS
LIMIT = 56 * 2**20
BF, F32 = jnp.bfloat16, jnp.float32


def along_z(k):
    return [
        (x * Z + z, x * Z + (z + HOP[k][z % 2]) % Z) for x in range(X) for z in range(Z)
    ]


def home(k, step, sections):
    n = X * Z
    return [
        (s * n + b, (s + step) % sections * n + a) for s in range(sections) for a, b in along_z(k)
    ]


def dot(a, b, dims=((1,), (0,))):
    return lax.dot_general(a, b, (dims, ((), ())), preferred_element_type=F32)


def call(kernel, outs, args, flops=0, scratch=(), hbm=(), after=()):
    moved = sum(a.size * a.dtype.itemsize for a in args) + sum(
        o.size * o.dtype.itemsize for o in outs
    )
    n = len(args)
    specs = [pl.BlockSpec(memory_space=pl.ANY if i in hbm else pltpu.VMEM) for i in range(n)]
    specs += [pl.BlockSpec(memory_space=pl.ANY)] * len(after)
    return pl.pallas_call(
        lambda *refs: kernel(*refs[:n], *refs[n + len(after) :]),
        out_shape=outs,
        in_specs=specs,
        out_specs=[pl.BlockSpec(memory_space=pltpu.VMEM)] * len(outs),
        scratch_shapes=list(scratch),
        compiler_params=pltpu.CompilerParams(vmem_limit_bytes=LIMIT),
        cost_estimate=pl.CostEstimate(flops=flops, bytes_accessed=moved, transcendentals=0),
    )(*args, *after)


def places(routes):
    count = routes.shape[0]
    z = lax.axis_index("z")
    same = routes[:, None] == routes[None, :]
    ids = jnp.arange(count, dtype=jnp.int32)
    earlier = ids[None, :] < ids[:, None]
    slot = jnp.sum((same & earlier).astype(jnp.int32), axis=1)
    dq = (routes % Q - z // 2 + Q) % Q
    odd = jnp.where(dq == 0, 0, dq % (Q - 1) + 1)
    k = jnp.where(z % 2 == 0, dq, odd)
    return (k * X + routes // Q) * CH + slot


def pack_kernel(units, tgt, *refs):
    tokens, outs = refs[:units], refs[units:]
    rows = len(HOP) * X * CH
    count, width = tokens[0].shape[1:]
    cut, part = width // CUTS, rows // len(HOP)
    at = lax.broadcasted_iota(jnp.int32, (rows, count), 0)
    t = tgt[...]
    pick = jnp.concatenate(
        [(at == t + cb * CAP).astype(F32).astype(BF) for cb in range(CUTS)], axis=1
    )
    for u, ref in enumerate(tokens):
        v = ref[0]
        stacked = jnp.concatenate([v[:, cb * cut : (cb + 1) * cut] for cb in range(CUTS)], axis=0)
        got = dot(pick, stacked).astype(BF)
        for k in range(len(HOP)):
            outs[u * len(HOP) + k][...] = got[k * part : (k + 1) * part]


def pack(tgt, tokens, after=()):
    count, width = tokens[0].shape[1:]
    units, cut = len(tokens), width // CUTS
    rows = len(HOP) * X * CH
    outs = [jax.ShapeDtypeStruct((X * CH, cut), BF)] * (units * len(HOP))
    got = call(
        lambda *r: pack_kernel(units, *r),
        outs,
        (tgt[None, :], *tokens),
        flops=2 * units * rows * count * CUTS * cut,
        after=after,
    )
    return [got[u * len(HOP) : (u + 1) * len(HOP)] for u in range(units)]


def by_column_kernel(*refs):
    ins, out = refs[:-1], refs[-1]
    for x in range(X):
        for k, r in enumerate(ins):
            out[x, k * CH : (k + 1) * CH, :] = r[x * CH : (x + 1) * CH, :]


def by_column(chunks, after=()):
    out = jax.ShapeDtypeStruct((X, len(chunks) * CH, chunks[0].shape[1]), BF)
    return call(by_column_kernel, [out], chunks, after=after)[0]


def by_route_kernel(columns, *outs):
    for k, out in enumerate(outs):
        for x in range(X):
            out[x * CH : (x + 1) * CH, :] = columns[x, k * CH : (k + 1) * CH, :]


def by_route(columns, after=()):
    outs = [jax.ShapeDtypeStruct((X * CH, columns.shape[2]), BF)] * len(HOP)
    return call(by_route_kernel, outs, (columns,), after=after)


def shuffle(rows, back):
    shape = (rows, rows)
    plain = lax.broadcasted_iota(jnp.int32, shape, 1 if back else 0)
    packed = lax.broadcasted_iota(jnp.int32, shape, 0 if back else 1)
    per = rows // CUTS
    block = plain // per
    chunk = (plain % per) // CAP
    slot = plain % CAP
    return (packed == chunk * CH + block * CAP + slot).astype(F32).astype(BF)


def depack_kernel(columns, out):
    n, part, cut = columns.shape
    rows, per = n * part, n * part // CUTS
    packed = jnp.concatenate([columns[i] for i in range(n)], axis=0)
    got = dot(shuffle(rows, False), packed).astype(BF)
    for cb in range(CUTS):
        out[:, cb * cut : (cb + 1) * cut] = got[cb * per : (cb + 1) * per]


def depack(columns, after=()):
    n, part, cut = columns.shape
    out = jax.ShapeDtypeStruct((n * part // CUTS, CUTS * cut), BF)
    return call(depack_kernel, [out], (columns,), flops=2 * (n * part) ** 2 * cut, after=after)[0]


def fetch(weights, bufs, sems):
    half = weights[3].shape[1]
    places = [bufs[0], bufs[1], bufs[2], bufs[3].at[:half], bufs[3].at[half:], bufs[4], bufs[5]]
    copies = [
        pltpu.make_async_copy(w.at[0], b, sems.at[i]) for i, (w, b) in enumerate(zip(weights, places))
    ]
    for c in copies:
        c.start()
    return copies


def forward_kernel(own, other, *refs):
    weights, (mine, theirs), bufs, sems = refs[:7], refs[7:9], refs[9:15], refs[15]
    copies = fetch(weights, bufs, sems)
    rows, width = own.shape
    x = jnp.concatenate([own[...], other[...]], axis=0)
    hidden = []
    for h, needs in enumerate(((0, 2), (1, 3, 4))):
        for i in needs:
            copies[i].wait()
        gate = dot(x, bufs[h][...])
        up = dot(x, bufs[2 + h][...])
        hidden.append((gate * jax.nn.sigmoid(gate) * up).astype(BF))
    copies[5].wait()
    copies[6].wait()
    cut = width // CUTS
    for cb in range(CUTS):
        cols = slice(cb * cut, (cb + 1) * cut)
        part = dot(hidden[0], bufs[4][:, cols]) + dot(hidden[1], bufs[5][:, cols])
        mine[:, cols] = part[:rows]
        theirs[:, cols] = part[rows:].astype(BF)


def early_kernel(x_own, x_other, g_own, *refs):
    weights, (gates, ups, carried), bufs, sems = refs[:7], refs[7:10], refs[10:16], refs[16]
    copies = fetch(weights, bufs, sems)
    x = jnp.concatenate([x_own[...], x_other[...]], axis=0)
    hid = bufs[0].shape[1]
    for h, needs in enumerate(((0, 2, 5), (1, 3, 4, 6))):
        for i in needs:
            copies[i].wait()
        cols = slice(h * hid, (h + 1) * hid)
        gates[:, cols] = dot(x, bufs[h][...])
        ups[:, cols] = dot(x, bufs[2 + h][...])
        carried[:, cols] = dot(g_own[...], bufs[4 + h][...], ((1,), (1,)))


def backward_kernel(g_other, gates, ups, carried, *refs):
    weights, (mine, theirs), bufs, sems = refs[:7], refs[7:9], refs[9:15], refs[15]
    copies = fetch(weights, bufs, sems)
    rows, width = g_other.shape
    hid = bufs[0].shape[1]
    copies[5].wait()
    copies[6].wait()
    back = []
    for h in range(2):
        cols = slice(h * hid, (h + 1) * hid)
        gate, up = gates[:, cols], ups[:, cols]
        theirs_carried = dot(g_other[...], bufs[4 + h][...], ((1,), (1,)))
        c = jnp.concatenate([carried[:, cols], theirs_carried], axis=0)
        sigma = jax.nn.sigmoid(gate)
        d_gate = (c * up * sigma * (1.0 + gate * (1.0 - sigma))).astype(BF)
        d_up = (c * gate * sigma).astype(BF)
        back.append((d_gate, d_up))
    for i in range(5):
        copies[i].wait()
    cut = width // CUTS
    for cb in range(CUTS):
        cols = slice(cb * cut, (cb + 1) * cut)
        part = None
        for h in range(2):
            for i in range(2):
                term = dot(back[h][i], bufs[2 * i + h][cols, :], ((1,), (1,)))
                part = term if part is None else part + term
        mine[:, cols] = part[:rows]
        theirs[:, cols] = part[rows:].astype(BF)


def experts(kernel, outs, rows, weights, products, after=()):
    whole = (0, 0, 0, 0, 5, 5)
    scratch = [pltpu.VMEM(weights[i].shape[1:], BF) for i in whole]
    n = len(rows)
    return call(
        kernel,
        outs,
        (*rows, *weights),
        flops=2 * products * X * len(HOP) * CAP * 4 * weights[0].size,
        scratch=scratch + [pltpu.SemaphoreType.DMA((7,))],
        hbm=range(n, n + 7),
        after=after,
    )


def add_kernel(mine, got, out):
    rows, width = mine.shape
    cut = width // CUTS
    total = (mine[...] + got[...].astype(F32)).astype(BF)
    stacked = jnp.concatenate([total[:, cb * cut : (cb + 1) * cut] for cb in range(CUTS)], axis=0)
    packed = dot(shuffle(rows * CUTS, True), stacked).astype(BF)
    part = rows * CUTS // X
    for x in range(X):
        out[x] = packed[x * part : (x + 1) * part]


def add(mine, got, after=()):
    rows, width = mine.shape
    out = jax.ShapeDtypeStruct((X, rows * CUTS // X, width // CUTS), BF)
    flops = 2 * (rows * CUTS) ** 2 * width // CUTS
    return call(add_kernel, [out], (mine, got), flops=flops, after=after)[0]


def unpack_kernel(tgt, mix, *refs):
    ins, out = refs[:-1], refs[-1]
    packed = jnp.concatenate([r[...] for r in ins], axis=0)
    rows, cut = packed.shape
    count = tgt.shape[0]
    at = lax.broadcasted_iota(jnp.int32, (count, rows), 1)
    t, w = tgt[...], mix[...]
    for cb in range(CUTS):
        pick = (at == t + cb * CAP).astype(F32).astype(BF)
        out[0, :, cb * cut : (cb + 1) * cut] = (dot(pick, packed) * w).astype(BF)


def unpack(tgt, mix, arrays):
    rows, cut = arrays[0].shape
    count = tgt.shape[0]
    out = jax.ShapeDtypeStruct((1, count, CUTS * cut), BF)
    return call(
        unpack_kernel,
        [out],
        (tgt, mix, *arrays),
        flops=2 * CUTS * count * len(arrays) * rows * cut,
    )[0]


def send(chunks):
    return [chunks[0]] + [
        lax.ppermute(chunks[k], ("x", "z"), along_z(k)) for k in range(1, len(HOP))
    ]


def across(columns):
    return lax.all_to_all(columns, "x", 0, 0, tiled=True)


def to_pair(rows):
    return lax.ppermute(rows, "z", [(z, z ^ 1) for z in range(Z)])


def to_narrow(w):
    return lax.ppermute(w, "narrow", [(0, 1), (1, 0)])


def held(array, *before):
    return lax.optimization_barrier((array, *before))[0]


def send_home(chunks, step):
    sections = lax.axis_size("section")
    return [
        lax.ppermute(chunks[k], ("section", "x", "z"), home(k, step, sections))
        for k in range(len(HOP))
    ]


def table(tgt, weights, step):
    count = lax.axis_size("section")
    both = jnp.stack([tgt.astype(F32), weights])
    both = lax.ppermute(both, "section", [(i, (i + step) % count) for i in range(count)])
    return both[0].astype(jnp.int32)[:, None], both[1][:, None]


def on_device(
    ahead_tokens,
    ahead_routes,
    ahead_weights,
    back_tokens,
    back_grads,
    back_routes,
    back_weights,
    gate_weight,
    up_weight,
    down_weight,
):
    ahead_tgt = places(ahead_routes[0, :, 0])
    back_tgt = places(back_routes[0, :, 0])
    half = up_weight.shape[1] // 2
    gate_1 = to_narrow(gate_weight)
    (ahead,) = pack(ahead_tgt, [ahead_tokens])
    back, grad = pack(back_tgt, [back_tokens, back_grads], [ahead[0]])

    packed = back[0]
    ahead = send(ahead)
    back = send([back[0]] + [held(c, a) for c, a in zip(back[1:], ahead[1:])])
    ahead = by_column(ahead, [gate_1, packed])
    up_1 = to_narrow(held(up_weight[:, :half], ahead))
    ahead_own = depack(across(ahead), [up_1])
    ahead_other = to_pair(ahead_own)

    up_2 = to_narrow(held(up_weight[:, half:], ahead_own))
    grad = send([grad[0]] + [held(c, b) for c, b in zip(grad[1:], back[1:])])
    back = by_column(back, [ahead_own])
    back_own = depack(across(back), [ahead_other, up_2, *grad[1:]])
    down_1 = to_narrow(held(down_weight, back_own))
    back_other = to_pair(back_own)

    grad = by_column(grad, [back_own])
    grad_own = depack(across(grad), [back_other])
    grad_other = to_pair(grad_own)

    rows, width = ahead_own.shape
    hid = 2 * down_weight.shape[1]
    weights = [gate_weight, gate_1, up_weight, up_1, up_2, down_weight, down_1]
    sums = [jax.ShapeDtypeStruct((rows, width), t) for t in (F32, BF)]
    mine, theirs = experts(forward_kernel, sums, [ahead_own, ahead_other], weights, 6, [grad_own])
    ahead_mine, ahead_got = mine, to_pair(theirs)

    outs = [jax.ShapeDtypeStruct((n, hid), F32) for n in (2 * rows, 2 * rows, rows)]
    inputs = [back_own, back_other, grad_own]
    early = experts(early_kernel, outs, inputs, weights, 5, [theirs])
    mine, theirs = experts(backward_kernel, sums, [grad_other, *early], weights, 5)

    ahead_table = table(ahead_tgt, ahead_weights[0, :, 0], 1)
    back_table = table(back_tgt, back_weights[0, :, 0], -1)
    ahead = add(ahead_mine, ahead_got, [theirs, *ahead_table, *back_table])
    ahead = by_route(across(ahead))
    back = add(mine, to_pair(theirs), [ahead[0]])
    ahead = send_home(ahead, 1)
    back = send_home(by_route(across(back)), -1)
    return unpack(*ahead_table, ahead), unpack(*back_table, back)


def solution(mesh):
    grid = Mesh(
        mesh.devices.reshape(mesh.shape["section"], X, Z, mesh.shape["narrow"]),
        ("section", "x", "z", "narrow"),
    )
    split = ("x", "z", "narrow")
    tokens = P("section", split, None)
    columns = P("section", None, split)
    in_specs = (tokens,) * 7 + (columns, columns, tokens)
    return jax.shard_map(
        on_device, mesh=grid, in_specs=in_specs, out_specs=(tokens, tokens), check_vma=False
    )
```

```python
import jax
import jax.numpy as jnp
from jax import lax
from jax.experimental import pallas as pl
from jax.experimental.pallas import tpu as pltpu
from jax.sharding import Mesh
from jax.sharding import PartitionSpec as P

X, Z = 4, 8
Q = Z // 2
HOP = ((0, 0), (2, 6), (5, 1), (7, 3))
CAP = 10
CUTS = 4
CH = CAP * CUTS
LIMIT = 56 * 2**20
BF, F32 = jnp.bfloat16, jnp.float32


def along_z(k):
    return [
        (x * Z + z, x * Z + (z + HOP[k][z % 2]) % Z) for x in range(X) for z in range(Z)
    ]


def home(k, step, sections):
    n = X * Z
    return [
        (s * n + b, (s + step) % sections * n + a) for s in range(sections) for a, b in along_z(k)
    ]


def dot(a, b, dims=((1,), (0,))):
    return lax.dot_general(a, b, (dims, ((), ())), preferred_element_type=F32)


def call(kernel, outs, args, flops=0, scratch=(), hbm=(), after=()):
    moved = sum(a.size * a.dtype.itemsize for a in args) + sum(
        o.size * o.dtype.itemsize for o in outs
    )
    n = len(args)
    specs = [pl.BlockSpec(memory_space=pl.ANY if i in hbm else pltpu.VMEM) for i in range(n)]
    specs += [pl.BlockSpec(memory_space=pl.ANY)] * len(after)
    return pl.pallas_call(
        lambda *refs: kernel(*refs[:n], *refs[n + len(after) :]),
        out_shape=outs,
        in_specs=specs,
        out_specs=[pl.BlockSpec(memory_space=pltpu.VMEM)] * len(outs),
        scratch_shapes=list(scratch),
        compiler_params=pltpu.CompilerParams(vmem_limit_bytes=LIMIT),
        cost_estimate=pl.CostEstimate(flops=flops, bytes_accessed=moved, transcendentals=0),
    )(*args, *after)


def places(routes):
    count = routes.shape[0]
    z = lax.axis_index("z")
    same = routes[:, None] == routes[None, :]
    ids = jnp.arange(count, dtype=jnp.int32)
    earlier = ids[None, :] < ids[:, None]
    slot = jnp.sum((same & earlier).astype(jnp.int32), axis=1)
    dq = (routes % Q - z // 2 + Q) % Q
    odd = jnp.where(dq == 0, 0, dq % (Q - 1) + 1)
    k = jnp.where(z % 2 == 0, dq, odd)
    return (k * X + routes // Q) * CH + slot


def pack_kernel(units, tgt, *refs):
    tokens, outs = refs[:units], refs[units:]
    rows = len(HOP) * X * CH
    count, width = tokens[0].shape[1:]
    cut, part = width // CUTS, rows // len(HOP)
    at = lax.broadcasted_iota(jnp.int32, (rows, count), 0)
    t = tgt[...]
    pick = jnp.concatenate(
        [(at == t + cb * CAP).astype(F32).astype(BF) for cb in range(CUTS)], axis=1
    )
    for u, ref in enumerate(tokens):
        v = ref[0]
        stacked = jnp.concatenate([v[:, cb * cut : (cb + 1) * cut] for cb in range(CUTS)], axis=0)
        got = dot(pick, stacked).astype(BF)
        for k in range(len(HOP)):
            outs[u * len(HOP) + k][...] = got[k * part : (k + 1) * part]


def pack(tgt, tokens, after=()):
    count, width = tokens[0].shape[1:]
    units, cut = len(tokens), width // CUTS
    rows = len(HOP) * X * CH
    outs = [jax.ShapeDtypeStruct((X * CH, cut), BF)] * (units * len(HOP))
    got = call(
        lambda *r: pack_kernel(units, *r),
        outs,
        (tgt[None, :], *tokens),
        flops=2 * units * rows * count * CUTS * cut,
        after=after,
    )
    return [got[u * len(HOP) : (u + 1) * len(HOP)] for u in range(units)]


def by_column_kernel(*refs):
    ins, out = refs[:-1], refs[-1]
    for x in range(X):
        for k, r in enumerate(ins):
            out[x, k * CH : (k + 1) * CH, :] = r[x * CH : (x + 1) * CH, :]


def by_column(chunks, after=()):
    out = jax.ShapeDtypeStruct((X, len(chunks) * CH, chunks[0].shape[1]), BF)
    return call(by_column_kernel, [out], chunks, after=after)[0]


def by_route_kernel(columns, *outs):
    for k, out in enumerate(outs):
        for x in range(X):
            out[x * CH : (x + 1) * CH, :] = columns[x, k * CH : (k + 1) * CH, :]


def by_route(columns, after=()):
    outs = [jax.ShapeDtypeStruct((X * CH, columns.shape[2]), BF)] * len(HOP)
    return call(by_route_kernel, outs, (columns,), after=after)


def shuffle(rows, back):
    shape = (rows, rows)
    plain = lax.broadcasted_iota(jnp.int32, shape, 1 if back else 0)
    packed = lax.broadcasted_iota(jnp.int32, shape, 0 if back else 1)
    per = rows // CUTS
    block = plain // per
    chunk = (plain % per) // CAP
    slot = plain % CAP
    return (packed == chunk * CH + block * CAP + slot).astype(F32).astype(BF)


def depack_kernel(columns, out):
    n, part, cut = columns.shape
    rows, per = n * part, n * part // CUTS
    packed = jnp.concatenate([columns[i] for i in range(n)], axis=0)
    got = dot(shuffle(rows, False), packed).astype(BF)
    for cb in range(CUTS):
        out[:, cb * cut : (cb + 1) * cut] = got[cb * per : (cb + 1) * per]


def depack(columns, after=()):
    n, part, cut = columns.shape
    out = jax.ShapeDtypeStruct((n * part // CUTS, CUTS * cut), BF)
    return call(depack_kernel, [out], (columns,), flops=2 * (n * part) ** 2 * cut, after=after)[0]


def fetch(weights, bufs, sems):
    copies = [
        pltpu.make_async_copy(w.at[0], b, sems.at[i]) for i, (w, b) in enumerate(zip(weights, bufs))
    ]
    for c in copies:
        c.start()
    return copies


def forward_kernel(own, other, *refs):
    weights, (mine, theirs), bufs, sems = refs[:6], refs[6:8], refs[8:14], refs[14]
    copies = fetch(weights, bufs, sems)
    rows, width = own.shape
    x = jnp.concatenate([own[...], other[...]], axis=0)
    hidden = []
    for h, needs in enumerate(((0, 2), (1, 3))):
        for i in needs:
            copies[i].wait()
        gate = dot(x, bufs[h][...])
        up = dot(x, bufs[2 + h][...])
        hidden.append((gate * jax.nn.sigmoid(gate) * up).astype(BF))
    copies[4].wait()
    copies[5].wait()
    cut = width // CUTS
    for cb in range(CUTS):
        cols = slice(cb * cut, (cb + 1) * cut)
        part = dot(hidden[0], bufs[4][:, cols]) + dot(hidden[1], bufs[5][:, cols])
        mine[:, cols] = part[:rows]
        theirs[:, cols] = part[rows:].astype(BF)


def early_kernel(x_own, x_other, g_own, *refs):
    weights, (gates, ups, carried), bufs, sems = refs[:6], refs[6:9], refs[9:15], refs[15]
    copies = fetch(weights, bufs, sems)
    x = jnp.concatenate([x_own[...], x_other[...]], axis=0)
    hid = bufs[0].shape[1]
    for h, needs in enumerate(((0, 2, 4), (1, 3, 5))):
        for i in needs:
            copies[i].wait()
        cols = slice(h * hid, (h + 1) * hid)
        gates[:, cols] = dot(x, bufs[h][...])
        ups[:, cols] = dot(x, bufs[2 + h][...])
        carried[:, cols] = dot(g_own[...], bufs[4 + h][...], ((1,), (1,)))


def backward_kernel(g_other, gates, ups, carried, *refs):
    weights, (mine, theirs), bufs, sems = refs[:6], refs[6:8], refs[8:14], refs[14]
    copies = fetch(weights, bufs, sems)
    rows, width = g_other.shape
    hid = bufs[0].shape[1]
    copies[4].wait()
    copies[5].wait()
    back = []
    for h in range(2):
        cols = slice(h * hid, (h + 1) * hid)
        gate, up = gates[:, cols], ups[:, cols]
        theirs_carried = dot(g_other[...], bufs[4 + h][...], ((1,), (1,)))
        c = jnp.concatenate([carried[:, cols], theirs_carried], axis=0)
        sigma = jax.nn.sigmoid(gate)
        d_gate = (c * up * sigma * (1.0 + gate * (1.0 - sigma))).astype(BF)
        d_up = (c * gate * sigma).astype(BF)
        back.append((d_gate, d_up))
    for i in range(4):
        copies[i].wait()
    cut = width // CUTS
    for cb in range(CUTS):
        cols = slice(cb * cut, (cb + 1) * cut)
        part = None
        for h in range(2):
            for i in range(2):
                term = dot(back[h][i], bufs[2 * i + h][cols, :], ((1,), (1,)))
                part = term if part is None else part + term
        mine[:, cols] = part[:rows]
        theirs[:, cols] = part[rows:].astype(BF)


def experts(kernel, outs, rows, weights, products, after=()):
    scratch = [pltpu.VMEM(w.shape[1:], BF) for w in weights]
    n = len(rows)
    return call(
        kernel,
        outs,
        (*rows, *weights),
        flops=2 * products * X * len(HOP) * CAP * 4 * weights[0].size,
        scratch=scratch + [pltpu.SemaphoreType.DMA((6,))],
        hbm=range(n, n + 6),
        after=after,
    )


def add_kernel(mine, got, out):
    rows, width = mine.shape
    cut = width // CUTS
    total = (mine[...] + got[...].astype(F32)).astype(BF)
    stacked = jnp.concatenate([total[:, cb * cut : (cb + 1) * cut] for cb in range(CUTS)], axis=0)
    packed = dot(shuffle(rows * CUTS, True), stacked).astype(BF)
    part = rows * CUTS // X
    for x in range(X):
        out[x] = packed[x * part : (x + 1) * part]


def add(mine, got, after=()):
    rows, width = mine.shape
    out = jax.ShapeDtypeStruct((X, rows * CUTS // X, width // CUTS), BF)
    flops = 2 * (rows * CUTS) ** 2 * width // CUTS
    return call(add_kernel, [out], (mine, got), flops=flops, after=after)[0]


def unpack_kernel(tgt, mix, *refs):
    ins, out = refs[:-1], refs[-1]
    packed = jnp.concatenate([r[...] for r in ins], axis=0)
    rows, cut = packed.shape
    count = tgt.shape[0]
    at = lax.broadcasted_iota(jnp.int32, (count, rows), 1)
    t, w = tgt[...], mix[...]
    for cb in range(CUTS):
        pick = (at == t + cb * CAP).astype(F32).astype(BF)
        out[0, :, cb * cut : (cb + 1) * cut] = (dot(pick, packed) * w).astype(BF)


def unpack(tgt, mix, arrays):
    rows, cut = arrays[0].shape
    count = tgt.shape[0]
    out = jax.ShapeDtypeStruct((1, count, CUTS * cut), BF)
    return call(
        unpack_kernel,
        [out],
        (tgt, mix, *arrays),
        flops=2 * CUTS * count * len(arrays) * rows * cut,
    )[0]


def send(chunks):
    return [chunks[0]] + [
        lax.ppermute(chunks[k], ("x", "z"), along_z(k)) for k in range(1, len(HOP))
    ]


def across(columns):
    return lax.all_to_all(columns, "x", 0, 0, tiled=True)


def to_pair(rows):
    return lax.ppermute(rows, "z", [(z, z ^ 1) for z in range(Z)])


def to_narrow(w):
    return lax.ppermute(w, "narrow", [(0, 1), (1, 0)])


def held(array, *before):
    return lax.optimization_barrier((array, *before))[0]


def send_home(chunks, step):
    sections = lax.axis_size("section")
    return [
        lax.ppermute(chunks[k], ("section", "x", "z"), home(k, step, sections))
        for k in range(len(HOP))
    ]


def table(tgt, weights, step):
    count = lax.axis_size("section")
    both = jnp.stack([tgt.astype(F32), weights])
    both = lax.ppermute(both, "section", [(i, (i + step) % count) for i in range(count)])
    return both[0].astype(jnp.int32)[:, None], both[1][:, None]


def on_device(
    ahead_tokens,
    ahead_routes,
    ahead_weights,
    back_tokens,
    back_grads,
    back_routes,
    back_weights,
    gate_weight,
    up_weight,
    down_weight,
):
    ahead_tgt = places(ahead_routes[0, :, 0])
    back_tgt = places(back_routes[0, :, 0])
    gate_1 = to_narrow(gate_weight)
    (ahead,) = pack(ahead_tgt, [ahead_tokens])
    back, grad = pack(back_tgt, [back_tokens, back_grads], [ahead[0]])

    packed = back[0]
    ahead = send(ahead)
    back = send([back[0]] + [held(c, a) for c, a in zip(back[1:], ahead[1:])])
    ahead = by_column(ahead, [gate_1, packed])
    up_1 = to_narrow(held(up_weight, ahead))
    ahead_own = depack(across(ahead))
    ahead_other = to_pair(ahead_own)

    grad = send([grad[0]] + [held(c, b) for c, b in zip(grad[1:], back[1:])])
    back = by_column(back, [ahead_own])
    down_1 = to_narrow(held(down_weight, back))
    back_own = depack(across(back), [ahead_other, up_1, *grad[1:]])
    back_other = to_pair(back_own)
    grad = across(by_column(grad, [back_own]))

    rows, width = ahead_own.shape
    hid = 2 * down_weight.shape[1]
    weights = [gate_weight, gate_1, up_weight, up_1, down_weight, down_1]
    sums = [jax.ShapeDtypeStruct((rows, width), t) for t in (F32, BF)]
    mine, theirs = experts(forward_kernel, sums, [ahead_own, ahead_other], weights, 6, [back_own])
    grad_own = depack(grad, [back_other, theirs])
    grad_other = to_pair(grad_own)
    ahead = add(mine, to_pair(theirs), [grad_own])

    outs = [jax.ShapeDtypeStruct((n, hid), F32) for n in (2 * rows, 2 * rows, rows)]
    early = experts(early_kernel, outs, [back_own, back_other, grad_own], weights, 5)
    mine, theirs = experts(backward_kernel, sums, [grad_other, *early], weights, 5, [ahead])

    ahead_table = table(held(ahead_tgt, early[0]), ahead_weights[0, :, 0], 1)
    back_table = table(held(back_tgt, early[0]), back_weights[0, :, 0], -1)
    ahead = by_route(across(ahead), [theirs])
    back = add(mine, to_pair(theirs), [ahead[0], *ahead_table, *back_table])
    ahead = send_home(ahead, 1)
    back = send_home(by_route(across(back)), -1)
    return unpack(*ahead_table, ahead), unpack(*back_table, back)


def solution(mesh):
    grid = Mesh(
        mesh.devices.reshape(mesh.shape["section"], X, Z, mesh.shape["narrow"]),
        ("section", "x", "z", "narrow"),
    )
    split = ("x", "z", "narrow")
    tokens = P("section", split, None)
    columns = P("section", None, split)
    in_specs = (tokens,) * 7 + (columns, columns, tokens)
    return jax.shard_map(
        on_device, mesh=grid, in_specs=in_specs, out_specs=(tokens, tokens), check_vma=False
    )
```

```python
import jax
import jax.numpy as jnp
from jax import lax
from jax.experimental import pallas as pl
from jax.experimental.pallas import tpu as pltpu
from jax.sharding import Mesh
from jax.sharding import PartitionSpec as P

X, Z = 4, 8
Q = Z // 2
HOP = ((0, 0), (2, 6), (5, 1), (7, 3))
CAP = 10
CUTS = 4
CH = CAP * CUTS
LIMIT = 56 * 2**20
BF, F32 = jnp.bfloat16, jnp.float32


def along_z(k):
    return [
        (x * Z + z, x * Z + (z + HOP[k][z % 2]) % Z) for x in range(X) for z in range(Z)
    ]


def home(k, step, sections):
    n = X * Z
    return [
        (s * n + b, (s + step) % sections * n + a) for s in range(sections) for a, b in along_z(k)
    ]


def dot(a, b, dims=((1,), (0,))):
    return lax.dot_general(a, b, (dims, ((), ())), preferred_element_type=F32)


def call(kernel, outs, args, flops=0, scratch=(), hbm=(), after=()):
    moved = sum(a.size * a.dtype.itemsize for a in args) + sum(
        o.size * o.dtype.itemsize for o in outs
    )
    n = len(args)
    specs = [pl.BlockSpec(memory_space=pl.ANY if i in hbm else pltpu.VMEM) for i in range(n)]
    specs += [pl.BlockSpec(memory_space=pl.ANY)] * len(after)
    return pl.pallas_call(
        lambda *refs: kernel(*refs[:n], *refs[n + len(after) :]),
        out_shape=outs,
        in_specs=specs,
        out_specs=[pl.BlockSpec(memory_space=pltpu.VMEM)] * len(outs),
        scratch_shapes=list(scratch),
        compiler_params=pltpu.CompilerParams(vmem_limit_bytes=LIMIT),
        cost_estimate=pl.CostEstimate(flops=flops, bytes_accessed=moved, transcendentals=0),
    )(*args, *after)


def places(routes):
    count = routes.shape[0]
    z = lax.axis_index("z")
    same = routes[:, None] == routes[None, :]
    ids = jnp.arange(count, dtype=jnp.int32)
    earlier = ids[None, :] < ids[:, None]
    slot = jnp.sum((same & earlier).astype(jnp.int32), axis=1)
    dq = (routes % Q - z // 2 + Q) % Q
    odd = jnp.where(dq == 0, 0, dq % (Q - 1) + 1)
    k = jnp.where(z % 2 == 0, dq, odd)
    return (k * X + routes // Q) * CH + slot


def pack_kernel(units, tgt, *refs):
    tokens, outs = refs[:units], refs[units:]
    rows = len(HOP) * X * CH
    count, width = tokens[0].shape[1:]
    cut, part = width // CUTS, rows // len(HOP)
    at = lax.broadcasted_iota(jnp.int32, (rows, count), 0)
    t = tgt[...]
    pick = jnp.concatenate(
        [(at == t + cb * CAP).astype(F32).astype(BF) for cb in range(CUTS)], axis=1
    )
    for u, ref in enumerate(tokens):
        v = ref[0]
        stacked = jnp.concatenate([v[:, cb * cut : (cb + 1) * cut] for cb in range(CUTS)], axis=0)
        got = dot(pick, stacked).astype(BF)
        for k in range(len(HOP)):
            outs[u * len(HOP) + k][...] = got[k * part : (k + 1) * part]


def pack(tgt, tokens, after=()):
    count, width = tokens[0].shape[1:]
    units, cut = len(tokens), width // CUTS
    rows = len(HOP) * X * CH
    outs = [jax.ShapeDtypeStruct((X * CH, cut), BF)] * (units * len(HOP))
    got = call(
        lambda *r: pack_kernel(units, *r),
        outs,
        (tgt[None, :], *tokens),
        flops=2 * units * rows * count * CUTS * cut,
        after=after,
    )
    return [got[u * len(HOP) : (u + 1) * len(HOP)] for u in range(units)]


def by_column_kernel(*refs):
    ins, out = refs[:-1], refs[-1]
    for x in range(X):
        for k, r in enumerate(ins):
            out[x, k * CH : (k + 1) * CH, :] = r[x * CH : (x + 1) * CH, :]


def by_column(chunks, after=()):
    out = jax.ShapeDtypeStruct((X, len(chunks) * CH, chunks[0].shape[1]), BF)
    return call(by_column_kernel, [out], chunks, after=after)[0]


def by_route_kernel(columns, *outs):
    for k, out in enumerate(outs):
        for x in range(X):
            out[x * CH : (x + 1) * CH, :] = columns[x, k * CH : (k + 1) * CH, :]


def by_route(columns, after=()):
    outs = [jax.ShapeDtypeStruct((X * CH, columns.shape[2]), BF)] * len(HOP)
    return call(by_route_kernel, outs, (columns,), after=after)


def shuffle(rows, back):
    shape = (rows, rows)
    plain = lax.broadcasted_iota(jnp.int32, shape, 1 if back else 0)
    packed = lax.broadcasted_iota(jnp.int32, shape, 0 if back else 1)
    per = rows // CUTS
    block = plain // per
    chunk = (plain % per) // CAP
    slot = plain % CAP
    return (packed == chunk * CH + block * CAP + slot).astype(F32).astype(BF)


def depack_kernel(columns, out):
    n, part, cut = columns.shape
    rows, per = n * part, n * part // CUTS
    packed = jnp.concatenate([columns[i] for i in range(n)], axis=0)
    got = dot(shuffle(rows, False), packed).astype(BF)
    for cb in range(CUTS):
        out[:, cb * cut : (cb + 1) * cut] = got[cb * per : (cb + 1) * per]


def depack(columns, after=()):
    n, part, cut = columns.shape
    out = jax.ShapeDtypeStruct((n * part // CUTS, CUTS * cut), BF)
    return call(depack_kernel, [out], (columns,), flops=2 * (n * part) ** 2 * cut, after=after)[0]


def fetch(weights, bufs, sems):
    copies = [
        pltpu.make_async_copy(w.at[0], b, sems.at[i]) for i, (w, b) in enumerate(zip(weights, bufs))
    ]
    for c in copies:
        c.start()
    return copies


def forward_kernel(own, other, *refs):
    weights, (mine, theirs), bufs, sems = refs[:6], refs[6:8], refs[8:14], refs[14]
    copies = fetch(weights, bufs, sems)
    rows, width = own.shape
    x = jnp.concatenate([own[...], other[...]], axis=0)
    hidden = []
    for h, needs in enumerate(((0, 2), (1, 3))):
        for i in needs:
            copies[i].wait()
        gate = dot(x, bufs[h][...])
        up = dot(x, bufs[2 + h][...])
        hidden.append((gate * jax.nn.sigmoid(gate) * up).astype(BF))
    copies[4].wait()
    copies[5].wait()
    cut = width // CUTS
    for cb in range(CUTS):
        cols = slice(cb * cut, (cb + 1) * cut)
        part = dot(hidden[0], bufs[4][:, cols]) + dot(hidden[1], bufs[5][:, cols])
        mine[:, cols] = part[:rows]
        theirs[:, cols] = part[rows:].astype(BF)


def early_kernel(x_own, x_other, g_own, *refs):
    weights, (gates, ups, carried), bufs, sems = refs[:6], refs[6:9], refs[9:15], refs[15]
    copies = fetch(weights, bufs, sems)
    x = jnp.concatenate([x_own[...], x_other[...]], axis=0)
    hid = bufs[0].shape[1]
    for h, needs in enumerate(((0, 2, 4), (1, 3, 5))):
        for i in needs:
            copies[i].wait()
        cols = slice(h * hid, (h + 1) * hid)
        gates[:, cols] = dot(x, bufs[h][...])
        ups[:, cols] = dot(x, bufs[2 + h][...])
        carried[:, cols] = dot(g_own[...], bufs[4 + h][...], ((1,), (1,)))


def backward_kernel(g_other, gates, ups, carried, *refs):
    weights, (mine, theirs), bufs, sems = refs[:6], refs[6:8], refs[8:14], refs[14]
    copies = fetch(weights, bufs, sems)
    rows, width = g_other.shape
    hid = bufs[0].shape[1]
    copies[4].wait()
    copies[5].wait()
    back = []
    for h in range(2):
        cols = slice(h * hid, (h + 1) * hid)
        gate, up = gates[:, cols], ups[:, cols]
        theirs_carried = dot(g_other[...], bufs[4 + h][...], ((1,), (1,)))
        c = jnp.concatenate([carried[:, cols], theirs_carried], axis=0)
        sigma = jax.nn.sigmoid(gate)
        d_gate = (c * up * sigma * (1.0 + gate * (1.0 - sigma))).astype(BF)
        d_up = (c * gate * sigma).astype(BF)
        back.append((d_gate, d_up))
    for i in range(4):
        copies[i].wait()
    cut = width // CUTS
    for cb in range(CUTS):
        cols = slice(cb * cut, (cb + 1) * cut)
        part = None
        for h in range(2):
            for i in range(2):
                term = dot(back[h][i], bufs[2 * i + h][cols, :], ((1,), (1,)))
                part = term if part is None else part + term
        mine[:, cols] = part[:rows]
        theirs[:, cols] = part[rows:].astype(BF)


def experts(kernel, outs, rows, weights, products, after=()):
    scratch = [pltpu.VMEM(w.shape[1:], BF) for w in weights]
    n = len(rows)
    return call(
        kernel,
        outs,
        (*rows, *weights),
        flops=2 * products * X * len(HOP) * CAP * 4 * weights[0].size,
        scratch=scratch + [pltpu.SemaphoreType.DMA((6,))],
        hbm=range(n, n + 6),
        after=after,
    )


def add_kernel(mine, got, out):
    rows, width = mine.shape
    cut = width // CUTS
    total = (mine[...] + got[...].astype(F32)).astype(BF)
    stacked = jnp.concatenate([total[:, cb * cut : (cb + 1) * cut] for cb in range(CUTS)], axis=0)
    packed = dot(shuffle(rows * CUTS, True), stacked).astype(BF)
    part = rows * CUTS // X
    for x in range(X):
        out[x] = packed[x * part : (x + 1) * part]


def add(mine, got, after=()):
    rows, width = mine.shape
    out = jax.ShapeDtypeStruct((X, rows * CUTS // X, width // CUTS), BF)
    flops = 2 * (rows * CUTS) ** 2 * width // CUTS
    return call(add_kernel, [out], (mine, got), flops=flops, after=after)[0]


def unpack_kernel(tgt, mix, *refs):
    ins, out = refs[:-1], refs[-1]
    packed = jnp.concatenate([r[...] for r in ins], axis=0)
    rows, cut = packed.shape
    count = tgt.shape[0]
    at = lax.broadcasted_iota(jnp.int32, (count, rows), 1)
    t, w = tgt[...], mix[...]
    for cb in range(CUTS):
        pick = (at == t + cb * CAP).astype(F32).astype(BF)
        out[0, :, cb * cut : (cb + 1) * cut] = (dot(pick, packed) * w).astype(BF)


def unpack(tgt, mix, arrays):
    rows, cut = arrays[0].shape
    count = tgt.shape[0]
    out = jax.ShapeDtypeStruct((1, count, CUTS * cut), BF)
    return call(
        unpack_kernel,
        [out],
        (tgt, mix, *arrays),
        flops=2 * CUTS * count * len(arrays) * rows * cut,
    )[0]


def send(chunks):
    return [chunks[0]] + [
        lax.ppermute(chunks[k], ("x", "z"), along_z(k)) for k in range(1, len(HOP))
    ]


def across(columns):
    return lax.all_to_all(columns, "x", 0, 0, tiled=True)


def to_pair(rows):
    return lax.ppermute(rows, "z", [(z, z ^ 1) for z in range(Z)])


def to_narrow(w):
    return lax.ppermute(w, "narrow", [(0, 1), (1, 0)])


def held(array, *before):
    return lax.optimization_barrier((array, *before))[0]


def send_home(chunks, step):
    sections = lax.axis_size("section")
    return [
        lax.ppermute(chunks[k], ("section", "x", "z"), home(k, step, sections))
        for k in range(len(HOP))
    ]


def table(tgt, weights, step):
    count = lax.axis_size("section")
    both = jnp.stack([tgt.astype(F32), weights])
    both = lax.ppermute(both, "section", [(i, (i + step) % count) for i in range(count)])
    return both[0].astype(jnp.int32)[:, None], both[1][:, None]


def on_device(
    ahead_tokens,
    ahead_routes,
    ahead_weights,
    back_tokens,
    back_grads,
    back_routes,
    back_weights,
    gate_weight,
    up_weight,
    down_weight,
):
    ahead_tgt = places(ahead_routes[0, :, 0])
    back_tgt = places(back_routes[0, :, 0])
    gate_1 = to_narrow(gate_weight)
    (ahead,) = pack(ahead_tgt, [ahead_tokens])
    back, grad = pack(back_tgt, [back_tokens, back_grads], [ahead[0]])

    packed = back[0]
    ahead = send(ahead)
    back = send([back[0]] + [held(c, a) for c, a in zip(back[1:], ahead[1:])])
    ahead = by_column(ahead, [gate_1, packed])
    up_1 = to_narrow(held(up_weight, ahead))
    ahead_own = depack(across(ahead))
    ahead_other = to_pair(ahead_own)

    grad = send([grad[0]] + [held(c, b) for c, b in zip(grad[1:], back[1:])])
    back = by_column(back, [ahead_own])
    down_1 = to_narrow(held(down_weight, back))
    back_own = depack(across(back), [ahead_other, up_1, *grad[1:]])
    back_other = to_pair(back_own)
    grad = across(by_column(grad, [back_own]))

    rows, width = ahead_own.shape
    hid = 2 * down_weight.shape[1]
    weights = [gate_weight, gate_1, up_weight, up_1, down_weight, down_1]
    sums = [jax.ShapeDtypeStruct((rows, width), t) for t in (F32, BF)]
    mine, theirs = experts(forward_kernel, sums, [ahead_own, ahead_other], weights, 6, [back_own])
    grad_own = depack(grad, [back_other, theirs])
    grad_other = to_pair(grad_own)
    ahead = add(mine, to_pair(theirs), [grad_own])

    outs = [jax.ShapeDtypeStruct((n, hid), F32) for n in (2 * rows, 2 * rows, rows)]
    early = experts(early_kernel, outs, [back_own, back_other, grad_own], weights, 5)
    ahead_table = table(held(ahead_tgt, early[0]), ahead_weights[0, :, 0], 1)
    back_table = table(held(back_tgt, early[0]), back_weights[0, :, 0], -1)
    ahead = by_route(across(ahead), [*ahead_table, *back_table])
    mine, theirs = experts(backward_kernel, sums, [grad_other, *early], weights, 5, [ahead[0]])
    ahead = send_home(ahead, 1)
    back = add(mine, to_pair(theirs), ahead)
    back = send_home(by_route(across(back)), -1)
    return unpack(*ahead_table, ahead), unpack(*back_table, back)


def solution(mesh):
    grid = Mesh(
        mesh.devices.reshape(mesh.shape["section"], X, Z, mesh.shape["narrow"]),
        ("section", "x", "z", "narrow"),
    )
    split = ("x", "z", "narrow")
    tokens = P("section", split, None)
    columns = P("section", None, split)
    in_specs = (tokens,) * 7 + (columns, columns, tokens)
    return jax.shard_map(
        on_device, mesh=grid, in_specs=in_specs, out_specs=(tokens, tokens), check_vma=False
    )
```
